1024 devices in a mesh: energy: 128 (over z, x), slab: 4 (over y_hi, core), rep: 2 (over y_lo).
Axes of the slice: x: 4, y: 4 (y_hi: 2, y_lo: 2; y = y_hi * 2 + y_lo), z: 32, core: 2. Of those that a mesh axis runs over, the one named last changes fastest.
Arguments:
- green_blocks: bfloat16 [128, 4, 512, 512], P('energy', 'slab', 'rep'), may hold values from -1 to 1
- occupation: float32 [128], P('energy'), may hold values from 0.1 to 1
- offsets: int32 [2], replicated, may hold values from 1 to 4, as said below
- coulomb: float32 [4, 512, 512], P('slab', 'rep'), may hold values from -0.9 to 0.9
- hamiltonian: float32 [4, 512, 512], P('slab', 'rep'), may hold values from -0.25 to 0.25
- onsite_level: float32 [128], P('energy'), may hold values from 2 to 3
- green_steps: int32 [128], P('energy'), may hold values from 1 to 2, as said below
- screen_steps: int32 [2], replicated, may hold values from 0 to 2, as said below
Outputs:
- green_next: float32 [128, 4, 512, 512], P('energy', 'slab', 'rep')
- screened: bfloat16 [2, 4, 512, 512], P(None, 'slab', 'rep')
The draws below stay inside these ranges and needn't reach their ends.
Inputs may be any that keep to these rules, and one draw needn't show every extreme that they name: `offsets`: some frequency has offset 4; every other frequency has a smaller one. `green_steps`: some energy takes 2 turns. `screen_steps`: some frequency takes 2 turns; every other frequency takes fewer.
All inputs are finite; a program needn't handle non-finite values.
Results may differ from the reference program's by a relative error of at most 0.0004.
Values may be sent and summed in bfloat16 or wider, within the bound.
A program may use at most 32 MiB of HBM per device.

```python
import math
import jax
import jax.numpy as jnp
from jax import lax

B = 512
SHIFTS = 4
FREQS = 2
NG = 2
NW = 2
E = 128
S = 4


def draw_offsets(key, part):
    own_key = jax.random.fold_in(key, 101)
    values = jax.random.randint(own_key, (FREQS,), 1, SHIFTS)
    place = jax.random.randint(jax.random.fold_in(own_key, 1), (), 0, FREQS)
    return values.at[place].set(SHIFTS).astype(jnp.int32)


def draw_green_steps(key, part):
    own_key = jax.random.fold_in(key, 202)
    values = jax.random.randint(own_key, (E,), 1, NG + 1)
    place = jax.random.randint(jax.random.fold_in(own_key, 1), (), 0, E)
    return values.at[place].set(NG).astype(jnp.int32)


def draw_screen_steps(key, part):
    own_key = jax.random.fold_in(key, 303)
    values = jax.random.randint(own_key, (FREQS,), 0, NW)
    place = jax.random.randint(jax.random.fold_in(own_key, 1), (), 0, FREQS)
    return values.at[place].set(NW).astype(jnp.int32)


def levels(key, shape, pieces, smallest, largest):
    def one(dim, blocks):
        steps = jax.random.uniform(jax.random.fold_in(jax.random.fold_in(key, 6), dim), (blocks,), jnp.float32, smallest / len(pieces), largest / len(pieces))
        return jnp.repeat(jnp.exp(steps), shape[dim] // blocks).reshape((-1,) + (1,) * (len(shape) - dim - 1))

    loudness = one(*pieces[0])
    for cut in pieces[1:]:
        loudness = loudness * one(*cut)
    return loudness


def noise(stream_key, extent, width, bound, split=(), kind=jnp.bfloat16):
    level = levels(stream_key, extent, split, -0.22, 0.18) if split else 1.0
    array = jax.random.normal(stream_key, extent, jnp.float32) * width * level
    return jnp.minimum(jnp.maximum(array, -bound), bound).astype(kind)


def setup_inputs(seed: int = 0) -> dict:
    key_of = jax.random.split(jax.random.key(seed), 9)
    green_blocks = jnp.clip(jax.random.uniform(key_of[0], (E, S, B, B), jnp.float32, -1.0, 1.0) * levels(key_of[0], (E, S, B, B), ((0, 128), (1, 4), (2, 2)), -0.4, 0.0), -1.0, 1.0).astype(jnp.bfloat16)
    occupation = jnp.clip(jnp.exp(math.log(1.0) - 2.3025851 * jax.random.uniform(key_of[1], (E,), jnp.float32) ** levels(key_of[1], (E,), ((0, 128),), -0.2, 0.2)), 0.1, 1.0)
    offsets = draw_offsets(jax.random.fold_in(key_of[8], 71), 0)
    coulomb = jnp.clip(jax.random.uniform(key_of[3], (S, B, B), jnp.float32, -0.9, 0.9) * levels(key_of[3], (S, B, B), ((0, 4), (1, 2)), -0.4, 0.0), -0.9, 0.9)
    hamiltonian = noise(key_of[4], (S, B, B), B ** -0.5, 0.25, ((0, 4), (1, 2)), jnp.float32)
    onsite_level = jnp.clip(2.0 + 1.0 * jax.random.uniform(key_of[5], (E,), jnp.float32) ** levels(key_of[5], (E,), ((0, 128),), -0.2, 0.2), 2.0, 3.0)
    green_steps = draw_green_steps(jax.random.fold_in(key_of[8], 71), 0)
    screen_steps = draw_screen_steps(jax.random.fold_in(key_of[8], 71), 0)
    return dict(green_blocks=green_blocks, occupation=occupation, offsets=offsets, coulomb=coulomb, hamiltonian=hamiltonian, onsite_level=onsite_level, green_steps=green_steps, screen_steps=screen_steps)


precise = lax.Precision.HIGHEST


def newton_solve(operator, initial, count, turn_total):
    iterate = initial
    for turn_index in range(turn_total):
        applied = jnp.matmul(operator, iterate, precision=precise)
        composed = jnp.matmul(iterate, applied, precision=precise)
        iterate = jnp.where(turn_index < count, 2.0 * iterate - composed, iterate)
    return iterate


def reference(green_blocks, occupation, offsets, coulomb, hamiltonian, onsite_level, green_steps, screen_steps):
    energies = green_blocks.shape[0]
    front = jnp.zeros((SHIFTS,) + green_blocks.shape[1:], green_blocks.dtype)
    padded = jnp.concatenate([front, green_blocks], axis=0)
    slab_padded = jnp.pad(green_blocks, ((0, 0), (1, 1), (0, 0), (0, 0)))
    identity = jnp.eye(B, dtype=jnp.float32)
    entry_scale = B ** -0.5

    def lowered_at(energy):
        blocks = [lax.dynamic_index_in_dim(padded, energy + SHIFTS - offsets[index], 0, keepdims=False) for index in range(FREQS)]
        return jnp.stack(blocks).astype(jnp.float32)

    def accumulate(total, energy):
        current = lax.dynamic_index_in_dim(green_blocks, energy, 0, keepdims=False).astype(jnp.float32)
        weighted = occupation[energy] * current
        return total + weighted[None] * lowered_at(energy), None

    zeros_total = jnp.zeros((FREQS,) + green_blocks.shape[1:], jnp.float32)
    polarization, _ = lax.scan(accumulate, zeros_total, jnp.arange(energies, dtype=jnp.int32))
    polarization = polarization * (energies ** -0.5)

    def screen_one(polar_slabs, count):
        operator = identity + entry_scale * coulomb * polar_slabs
        initial = jnp.broadcast_to(identity, operator.shape)
        inverse = newton_solve(operator, initial, count, NW)
        return jnp.matmul(coulomb, inverse, precision=precise).astype(jnp.bfloat16)

    screened = jnp.stack([screen_one(polarization[index], screen_steps[index]) for index in range(FREQS)])

    def solve_energy(energy):
        lowered = lowered_at(energy)
        self_energy = jnp.sum(lowered * screened.astype(jnp.float32), axis=0) * entry_scale
        beside_all = lax.dynamic_index_in_dim(slab_padded, energy, 0, keepdims=False)
        contact = (beside_all[:-2].astype(jnp.float32) + beside_all[2:].astype(jnp.float32)) * (0.5 * entry_scale)
        dyson = onsite_level[energy] * identity + hamiltonian - self_energy - contact
        diagonal = jnp.diagonal(dyson, axis1=1, axis2=2)
        initial = identity[None] * (1.0 / diagonal)[:, None, :]
        return newton_solve(dyson, initial, green_steps[energy], NG)

    green_next = lax.map(solve_energy, jnp.arange(energies, dtype=jnp.int32))
    return green_next, screened
```

```python
import functools
import jax
import jax.numpy as jnp
from jax import lax
from jax.sharding import PartitionSpec as P
import jax.experimental.pallas as pl
import jax.experimental.pallas.tpu as pltpu

MESH = pl.DeviceIdType.MESH
B = 512
H = 256
XN = 4
ZN = 32
E = XN * ZN
F32 = jnp.float32
BF16 = jnp.bfloat16


def split(value):
    high = value.astype(BF16)
    low = (value - high.astype(F32)).astype(BF16)
    return high, low


def dot(a, b):
    return jnp.dot(a, b, preferred_element_type=F32)


def product(first, high, low):
    fh, fl = split(first)
    return dot(fh, high) + (dot(fh, low) + dot(fl, high))


def kernel(
    occ_ref, off_ref, level_ref, gsteps_ref, ssteps_ref, g_ref, c_ref, h_ref,
    out_ref, w_ref,
    gbuf, occbuf, low, con, csib, part, right, left, shard, nblk, nhi, nlo, wown, wbuf,
    kf, kbuf, inv, zbuf,
    p_s, p_r, o_s, o_r, low_s, low_r, con_s, con_r, cs_s, cs_r, rr_s, rr_r, rl_s, rl_r,
    m_s, m_r, ar_s, ar_r, al_s, al_r, b_s, b_r, sib_s, sib_r, w_s, w_r, k_s, k_r, i_s, i_r,
):
    energy = lax.axis_index("energy")
    slab = lax.axis_index("slab")
    rep = lax.axis_index("rep")
    x, z = energy % XN, energy // XN
    yh, core = slab // 2, slab % 2
    zc, zb = z % 4, z // 4
    xh, xl = x // 2, x % 2

    def device(dx=0, dz=0, yh_=None, core_=None, rep_=None, x_=None):
        xx = (x + dx + XN) % XN if x_ is None else x_
        zz = (z + dz + ZN) % ZN
        yy = yh if yh_ is None else yh_
        cc = core if core_ is None else core_
        rr = rep if rep_ is None else rep_
        return (zz * XN + xx, yy * 2 + cc, rr)

    def remote(src, dst, send, recv, dev):
        return pltpu.make_async_remote_copy(
            src_ref=src, dst_ref=dst, send_sem=send, recv_sem=recv,
            device_id=dev, device_id_type=MESH,
        )

    def arrived(dst, send, recv):
        remote(dst, dst, send, recv, device(dx=1)).wait_recv()

    pending = []

    def go(*args):
        copy = remote(*args)
        copy.start()
        pending.append(copy)

    barrier = pltpu.get_barrier_semaphore()
    peers = [
        device(dx=dx, core_=(core + dc) % 2, rep_=(rep + dr) % 2)
        for dx in range(4) for dc in range(2) for dr in range(2) if (dx, dc, dr) != (0, 0, 0)
    ]
    peers += [device(dx=dx, dz=dz) for dz in (1, -1, 2, -2) for dx in range(4)]
    peers += [device(dz=4), device(dz=-4), device(yh_=1 - yh, core_=1 - core)]
    for dev in peers:
        pl.semaphore_signal(barrier, inc=1, device_id=dev, device_id_type=MESH)
    occbuf[0] = jnp.full((8, 128), occ_ref[0], F32)
    pl.semaphore_wait(barrier, len(peers))

    for slot in (0, 4, 1, 3, 2):
        dz = 2 - slot
        for dx in range(4):
            if dz == 0 and dx == 0:
                continue
            xd = (x + dx) % XN
            row = 4 * ((z + dz + ZN) % 4) + xd
            go(g_ref.at[row], gbuf.at[slot * 4 + x], p_s.at[slot, dx], p_r.at[slot, dx],
               device(dx=dx, dz=dz))
            if slot > 0:
                go(occbuf.at[0], occbuf.at[slot * 4 + x], o_s.at[slot, dx], o_r.at[slot, dx],
                   device(dx=dx, dz=dz))
    gbuf[8 + x] = g_ref[4 * zc + x]
    occbuf[8 + x] = jnp.full((8, 128), occ_ref[0], F32)
    go(g_ref, con.at[0], con_s.at[0], con_r.at[0], device(core_=1 - core))
    go(g_ref, con.at[1], con_s.at[1], con_r.at[1], device(yh_=1 - yh, core_=1 - core))
    go(c_ref.at[1 - core], csib, cs_s.at[0], cs_r.at[0], device(core_=1 - core))

    for slot in range(5):
        for dx in range(4):
            if slot == 2 and dx == 0:
                continue
            src_x = (x - dx + XN) % XN
            arrived(gbuf.at[slot * 4 + src_x], p_s.at[slot, dx], p_r.at[slot, dx])
            if slot > 0:
                arrived(occbuf.at[slot * 4 + src_x], o_s.at[slot, dx], o_r.at[slot, dx])

    offs = [jnp.clip(off_ref[f], 1, 4) for f in range(2)]

    def add_energy(n, carry):
        ee = 4 * ((z + n // 4 - 2 + ZN) % ZN) + n % 4
        cur = gbuf[n].astype(F32) * occbuf[n][0:1, 0:1]
        res = []
        for f in range(2):
            lowered = gbuf[n - offs[f]].astype(F32)
            valid = jnp.where(ee >= offs[f], 1.0, 0.0).astype(F32)
            res.append(carry[f] + cur * (lowered * valid))
        return tuple(res)

    zero = jnp.zeros((16, B), F32)
    acc = lax.fori_loop(4, 20, add_energy, (zero, zero))
    for f in range(2):
        for cb in range(4):
            part[4 * ((f + xh) % 2) + cb] = acc[f][:, 128 * cb:128 * cb + 128]

    for s in range(4):
        tr = (zb + 4 - s) % 8
        if s == 0:
            go(part.at[tr], right.at[0], rr_s.at[0], rr_r.at[0], device(dz=4))
        else:
            arrived(right.at[s - 1], rr_s.at[s - 1], rr_r.at[s - 1])
            right[s - 1] = right[s - 1] + part[tr]
            go(right.at[s - 1], right.at[s], rr_s.at[s], rr_r.at[s], device(dz=4))
        if s < 3:
            tl = (zb + 5 + s) % 8
            if s == 0:
                go(part.at[tl], left.at[0], rl_s.at[0], rl_r.at[0], device(dz=-4))
            else:
                arrived(left.at[s - 1], rl_s.at[s - 1], rl_r.at[s - 1])
                left[s - 1] = left[s - 1] + part[tl]
                go(left.at[s - 1], left.at[s], rl_s.at[s], rl_r.at[s], device(dz=-4))
        d = 4 - s
        up = energy + d
        up = jnp.where(up >= E, up - E, up)
        go(g_ref, low.at[d - 1], low_s.at[d - 1], low_r.at[d - 1], (up, slab, rep))
    arrived(left.at[2], rl_s.at[2], rl_r.at[2])
    arrived(right.at[3], rr_s.at[3], rr_r.at[3])
    total = (right[3] + left[2] + part[zb]) * (E ** -0.5)

    ft = (zb // 4 + xh) % 2
    row16 = 4 * zc + x
    c_rows = c_ref[row16 // 8, pl.ds(pl.multiple_of((row16 % 8) * 16, 16), 16),
                   pl.ds(pl.multiple_of((zb % 4) * 128, 128), 128)]
    sh, sl = split((B ** -0.5) * c_rows * total)
    shard[0] = sh
    shard[1] = sl
    xt = 2 * ft + core
    slot_n = nblk.at[rep, zc, zb, xl]
    own = jnp.logical_and(xt == x, core == rep)
    self_copy = pltpu.make_async_copy(shard, slot_n, m_r.at[xl])
    same_copy = remote(shard, slot_n, m_s.at[0], m_r.at[xl], device(x_=xt, core_=rep))
    pl.when(own)(self_copy.start)
    pl.when(jnp.logical_not(own))(same_copy.start)
    go(shard, slot_n, m_s.at[1], m_r.at[xl], device(x_=xt, core_=rep, rep_=1 - rep))
    for xs in range(2):
        arrived(nblk.at[core, zc, zb, xs], m_s.at[0], m_r.at[xs])

    dirs = (1, -1, 2)

    def to_window(block, index):
        for di, dz in enumerate(dirs):
            go(block, block, b_s.at[di, index], b_r.at[di, index], device(dz=dz))

    mine = nblk.at[core, zc, zb]
    go(mine, mine, ar_s.at[0], ar_r.at[0], device(dz=4))
    go(mine, mine, al_s.at[0], al_r.at[0], device(dz=-4))
    to_window(mine, 0)
    for s in range(4):
        block = nblk.at[core, zc, (zb + 7 - s) % 8]
        arrived(block, ar_s.at[s], ar_r.at[s])
        if s < 3:
            go(block, block, ar_s.at[s + 1], ar_r.at[s + 1], device(dz=4))
        to_window(block, 1 + s)
        if s < 3:
            block = nblk.at[core, zc, (zb + 1 + s) % 8]
            arrived(block, al_s.at[s], al_r.at[s])
            if s < 2:
                go(block, block, al_s.at[s + 1], al_r.at[s + 1], device(dz=-4))
            to_window(block, 5 + s)
    sibling = device(core_=1 - core)
    go(nblk.at[core, zc], nblk.at[core, zc], sib_s.at[0], sib_r.at[0], sibling)
    for di, dz in enumerate(dirs):
        zs = (z - dz + ZN) % ZN
        ks, js = zs // 4, zs % 4
        for index in range(8):
            kk = (ks + 8 - index if index < 5 else ks + index - 4) % 8
            arrived(nblk.at[core, js, kk], b_s.at[di, index], b_r.at[di, index])
        go(nblk.at[core, js], nblk.at[core, js], sib_s.at[1 + di], sib_r.at[1 + di], sibling)
    for n, dz in enumerate((0,) + dirs):
        js = (z - dz + ZN) % 4
        arrived(nblk.at[1 - core, js], sib_s.at[n], sib_r.at[n])

    def assemble(n, _):
        for p in range(2):
            for xs in range(2):
                for cb in range(4):
                    kk = 4 * ((xh + p) % 2) + cb
                    rows = pl.ds(pl.multiple_of(n * 64 + 32 * p + 16 * xs, 16), 16)
                    nhi[rows, 128 * cb:128 * cb + 128] = nblk[n // 4, n % 4, kk, xs, 0]
                    nlo[rows, 128 * cb:128 * cb + 128] = nblk[n // 4, n % 4, kk, xs, 1]
        return 0

    lax.fori_loop(0, 8, assemble, 0)

    arrived(csib, cs_s.at[0], cs_r.at[0])
    local = xl == core
    cw = jnp.where(local, c_ref[core], csib[...])
    count = ssteps_ref[xh]
    u1 = product(cw, nhi[...], nlo[...])
    u2 = product(u1, nhi[...], nlo[...])
    u3 = product(u2, nhi[...], nlo[...])
    w1 = cw - u1
    w2 = w1 + (u2 - u3)
    wown[...] = jnp.where(count >= 2, w2, jnp.where(count >= 1, w1, cw)).astype(BF16)
    slot_w = wbuf.at[xh, core]
    w_self = pltpu.make_async_copy(wown, slot_w, w_r.at[xh, core])
    w_sib = remote(wown, slot_w, w_s.at[0], w_r.at[xh, core], device(core_=xl))
    for dx in (1, 3, 2):
        go(wown, slot_w, w_s.at[dx], w_r.at[xh, core], device(dx=dx, core_=xl))
    pl.when(local)(w_self.start)
    pl.when(jnp.logical_not(local))(w_sib.start)

    for d in range(4):
        arrived(low.at[d], low_s.at[d], low_r.at[d])
    for n in range(2):
        arrived(con.at[n], con_s.at[n], con_r.at[n])
    for f in range(2):
        for half in range(2):
            arrived(wbuf.at[f, half], w_s.at[0], w_r.at[f, half])

    scale = B ** -0.5
    valid = [jnp.where(energy >= offs[f], scale, 0.0).astype(F32) for f in range(2)]
    inside = jnp.where(jnp.logical_or(slab == 0, slab == 3), 0.0, 0.5 * scale).astype(F32)
    level = level_ref[0]
    lane = lax.broadcasted_iota(jnp.int32, (32, B), 1)
    line = lax.broadcasted_iota(jnp.int32, (32, B), 0) + rep * H

    def operator(n, carry):
        pair = pl.ds(2 * n, 2)
        rows = pl.ds(pl.multiple_of(n * 32, 32), 32)
        half_rows = pl.ds(pl.multiple_of((n % 4) * 32, 32), 32)
        diag = lane == line + n * 32
        self_energy = jnp.zeros((32, B), F32)
        for f in range(2):
            lw = low[offs[f] - 1, pair].reshape(32, B).astype(F32)
            wf = wbuf[f, n // 4, half_rows, :].astype(F32)
            self_energy = self_energy + lw * wf * valid[f]
        contact = (con[0, pair].reshape(32, B).astype(F32) * (0.5 * scale)
                   + con[1, pair].reshape(32, B).astype(F32) * inside)
        dyson = jnp.where(diag, level, 0.0) + h_ref[rows, :] - self_energy - contact
        dd = jnp.sum(jnp.where(diag, dyson, 0.0), axis=1, keepdims=True)
        iv = 1.0 / dd
        kk = jnp.where(diag, 0.0, dyson * iv)
        kf[rows, :] = kk
        kh, kl = split(kk)
        kbuf[rep, 0, rows, :] = kh
        kbuf[rep, 1, rows, :] = kl
        return carry + jnp.sum(jnp.where(diag, iv, 0.0), axis=0, keepdims=True)

    inv_row = lax.fori_loop(0, 8, operator, jnp.zeros((1, B), F32))
    inv[0] = jnp.broadcast_to(inv_row, (8, B))
    partner = device(rep_=1 - rep)
    go(kbuf.at[rep], kbuf.at[rep], k_s.at[0], k_r.at[0], partner)
    go(inv.at[0], inv.at[1], i_s.at[0], i_r.at[0], partner)
    for f in range(2):
        for half in range(2):
            w_ref[f, 128 * half:128 * half + 128, :] = wbuf[f, half]

    def columns(r):
        return pl.ds(pl.multiple_of(r * H, H), H)

    def partial(r):
        return product(kf[:, columns(r)], kbuf[r, 0], kbuf[r, 1])

    zbuf[...] = partial(rep)
    arrived(kbuf.at[1 - rep], k_s.at[0], k_r.at[0])
    arrived(inv.at[1], i_s.at[0], i_r.at[0])
    zbuf[...] = zbuf[...] + partial(1 - rep)
    cube = (product(zbuf[:, 0:H], kbuf[0, 0], kbuf[0, 1])
            + product(zbuf[:, H:B], kbuf[1, 0], kbuf[1, 1]))
    inv_all = inv[0][0:1, :] + inv[1][0:1, :]
    twice = gsteps_ref[0] >= 2
    full_lane = lax.broadcasted_iota(jnp.int32, (H, B), 1)
    full_line = lax.broadcasted_iota(jnp.int32, (H, B), 0) + rep * H
    ident = jnp.where(full_lane == full_line, 1.0, 0.0).astype(F32)
    first = ident - kf[...]
    out_ref[...] = jnp.where(twice, first + (zbuf[...] - cube), first) * inv_all

    for copy in pending:
        copy.wait_send()
    pl.when(jnp.logical_not(own))(same_copy.wait_send)
    pl.when(jnp.logical_not(local))(w_sib.wait_send)


def body(green_blocks, occupation, offsets, coulomb, hamiltonian, onsite_level, green_steps,
         screen_steps):
    smem = pl.BlockSpec(memory_space=pltpu.SMEM)
    vmem = pl.BlockSpec(memory_space=pltpu.VMEM)
    dma = pltpu.SemaphoreType.DMA
    sems = []
    for shape in ((5, 4), (5, 4), (4,), (2,), (1,), (4,), (3,), (2,), (4,), (3,), (3, 8), (4,)):
        sems += [dma(shape), dma(shape)]
    sems += [dma((4,)), dma((2, 2)), dma((1,)), dma((1,)), dma((1,)), dma((1,))]
    green, screened = pl.pallas_call(
        kernel,
        out_shape=(
            jax.ShapeDtypeStruct((H, B), F32),
            jax.ShapeDtypeStruct((2, H, B), BF16),
        ),
        in_specs=[smem] * 5 + [vmem] * 3,
        out_specs=(vmem, vmem),
        scratch_shapes=[
            pltpu.VMEM((20, 16, B), BF16),
            pltpu.VMEM((20, 8, 128), F32),
            pltpu.VMEM((4, 16, 16, B), BF16),
            pltpu.VMEM((2, 16, 16, B), BF16),
            pltpu.VMEM((128, B), F32),
            pltpu.VMEM((8, 16, 128), F32),
            pltpu.VMEM((4, 16, 128), F32),
            pltpu.VMEM((3, 16, 128), F32),
            pltpu.VMEM((2, 16, 128), BF16),
            pltpu.VMEM((2, 4, 8, 2, 2, 16, 128), BF16),
            pltpu.VMEM((B, B), BF16),
            pltpu.VMEM((B, B), BF16),
            pltpu.VMEM((128, B), BF16),
            pltpu.VMEM((2, 2, 128, B), BF16),
            pltpu.VMEM((H, B), F32),
            pltpu.VMEM((2, 2, H, B), BF16),
            pltpu.VMEM((2, 8, B), F32),
            pltpu.VMEM((H, B), F32),
        ] + sems,
        compiler_params=pltpu.CompilerParams(
            collective_id=0, has_side_effects=True, vmem_limit_bytes=40 << 20
        ),
        name="gw_step",
    )(
        occupation, offsets, onsite_level, green_steps, screen_steps,
        green_blocks.reshape(16, 16, B), coulomb.reshape(2, 128, B), hamiltonian.reshape(H, B),
    )
    return green.reshape(1, 1, H, B), screened.reshape(2, 1, H, B)


def solution(mesh):
    return jax.shard_map(
        body,
        mesh=mesh,
        in_specs=(
            P("energy", "slab", "rep", None),
            P("energy"),
            P(),
            P("slab", "rep", None),
            P("slab", "rep", None),
            P("energy"),
            P("energy"),
            P(),
        ),
        out_specs=(P("energy", "slab", "rep", None), P(None, "slab", "rep", None)),
        check_vma=False,
    )
```

```python
import functools
import jax
import jax.numpy as jnp
from jax import lax
from jax.sharding import PartitionSpec as P
import jax.experimental.pallas as pl
import jax.experimental.pallas.tpu as pltpu

MESH = pl.DeviceIdType.MESH
B = 512
H = 256
XN = 4
ZN = 32
E = XN * ZN
F32 = jnp.float32
BF16 = jnp.bfloat16


def split(value):
    high = value.astype(BF16)
    low = (value - high.astype(F32)).astype(BF16)
    return high, low


def dot(a, b):
    return jnp.dot(a, b, preferred_element_type=F32)


def product(first, high, low):
    fh, fl = split(first)
    return dot(fh, high) + (dot(fh, low) + dot(fl, high))


def kernel(
    occ_ref, off_ref, level_ref, gsteps_ref, ssteps_ref, g_any, c_any, h_any,
    out_ref, w_ref,
    g_ref, c_ref, h_ref, gbuf, occbuf, low, con, csib, part, rs, shard, nblk, nhi, nlo, wown, wbuf,
    kf, kbuf, inv, zbuf,
    p_s, p_r, o_s, o_r, low_s, low_r, con_s, con_r, cs_s, cs_r, rs_s, rs_r,
    m_s, m_r, f_s, f_r, b_s, b_r, sib_s, sib_r, w_s, w_r, k_s, k_r, i_s, i_r, in_s, tok,
):
    energy = lax.axis_index("energy")
    slab = lax.axis_index("slab")
    rep = lax.axis_index("rep")
    x, z = energy % XN, energy // XN
    yh, core = slab // 2, slab % 2
    zc, zb = z % 4, z // 4
    xh, xl = x // 2, x % 2

    def device(dx=0, dz=0, yh_=None, core_=None, rep_=None, x_=None):
        xx = (x + dx + XN) % XN if x_ is None else x_
        zz = (z + dz + ZN) % ZN
        yy = yh if yh_ is None else yh_
        cc = core if core_ is None else core_
        rr = rep if rep_ is None else rep_
        return (zz * XN + xx, yy * 2 + cc, rr)

    def remote(src, dst, send, recv, dev):
        return pltpu.make_async_remote_copy(
            src_ref=src, dst_ref=dst, send_sem=send, recv_sem=recv,
            device_id=dev, device_id_type=MESH,
        )

    def arrived(dst, send, recv):
        remote(dst, dst, send, recv, device(dx=1)).wait_recv()

    pending = []

    def go(*args):
        copy = remote(*args)
        copy.start()
        pending.append(copy)

    load_g = pltpu.make_async_copy(g_any, g_ref, in_s.at[0])
    load_c = pltpu.make_async_copy(c_any, c_ref, in_s.at[1])
    load_h = pltpu.make_async_copy(h_any, h_ref, in_s.at[2])
    load_g.start()

    barrier = pltpu.get_barrier_semaphore()
    peers = [
        device(dx=dx, core_=(core + dc) % 2, rep_=(rep + dr) % 2)
        for dx in range(4) for dc in range(2) for dr in range(2) if (dx, dc, dr) != (0, 0, 0)
    ]
    peers += [device(dx=dx, dz=dz) for dz in (1, -1, 2, -2) for dx in range(4)]
    peers += [device(dz=4), device(dz=-4), device(yh_=1 - yh, core_=1 - core)]
    for dev in peers:
        pl.semaphore_signal(barrier, inc=1, device_id=dev, device_id_type=MESH)
    occbuf[0] = jnp.full((8, 128), occ_ref[0], F32)
    load_c.start()
    load_h.start()
    load_g.wait()
    pl.semaphore_wait(barrier, len(peers))
    for dz in (4, -4):
        pl.semaphore_signal(tok, inc=1, device_id=device(dz=dz), device_id_type=MESH)

    for slot in (0, 4, 1, 3, 2):
        dz = 2 - slot
        for dx in range(4):
            if dz == 0 and dx == 0:
                continue
            xd = (x + dx) % XN
            row = 4 * ((z + dz + ZN) % 4) + xd
            go(g_ref.at[row], gbuf.at[slot * 4 + x], p_s.at[slot, dx], p_r.at[slot, dx],
               device(dx=dx, dz=dz))
            if slot > 0:
                go(occbuf.at[0], occbuf.at[slot * 4 + x], o_s.at[slot, dx], o_r.at[slot, dx],
                   device(dx=dx, dz=dz))
    go(g_ref, low.at[3], low_s.at[3], low_r.at[3], device(dz=1))
    gbuf[8 + x] = g_ref[4 * zc + x]
    occbuf[8 + x] = jnp.full((8, 128), occ_ref[0], F32)
    go(g_ref, con.at[0], con_s.at[0], con_r.at[0], device(core_=1 - core))
    go(g_ref, con.at[1], con_s.at[1], con_r.at[1], device(yh_=1 - yh, core_=1 - core))
    load_c.wait()
    go(c_ref.at[1 - core], csib, cs_s.at[0], cs_r.at[0], device(core_=1 - core))

    for slot in range(5):
        for dx in range(4):
            if slot == 2 and dx == 0:
                continue
            src_x = (x - dx + XN) % XN
            arrived(gbuf.at[slot * 4 + src_x], p_s.at[slot, dx], p_r.at[slot, dx])
            if slot > 0:
                arrived(occbuf.at[slot * 4 + src_x], o_s.at[slot, dx], o_r.at[slot, dx])

    offs = [jnp.clip(off_ref[f], 1, 4) for f in range(2)]

    def add_energy(n, carry):
        ee = 4 * ((z + n // 4 - 2 + ZN) % ZN) + n % 4
        cur = gbuf[n].astype(F32) * occbuf[n][0:1, 0:1]
        res = []
        for f in range(2):
            lowered = gbuf[n - offs[f]].astype(F32)
            valid = jnp.where(ee >= offs[f], 1.0, 0.0).astype(F32)
            res.append(carry[f] + cur * (lowered * valid))
        return tuple(res)

    zero = jnp.zeros((16, B), F32)
    acc = lax.fori_loop(4, 20, add_energy, (zero, zero))
    for f in range(2):
        for cb in range(4):
            part[4 * ((f + xh) % 2) + cb] = acc[f][:, 128 * cb:128 * cb + 128]

    def shard_of(shift):
        return (zb + shift + 8) % 8

    pl.semaphore_wait(tok, 2)
    go(part.at[shard_of(4)], rs.at[0], rs_s.at[0], rs_r.at[0], device(dz=8))
    go(part.at[shard_of(3)], rs.at[1], rs_s.at[1], rs_r.at[1], device(dz=8))
    go(part.at[shard_of(-3)], rs.at[2], rs_s.at[2], rs_r.at[2], device(dz=-8))
    go(part.at[shard_of(-2)], rs.at[3], rs_s.at[3], rs_r.at[3], device(dz=-8))

    def to_row(dx, src):
        return remote(src, low.at[dx - 1], low_s.at[dx - 1], low_r.at[dx - 1], device(dx=dx))

    for dx in (1, 2, 3):
        pl.when(x + dx < XN)(to_row(dx, g_ref).start)

    for buf, shift, dst, dz in ((0, 2, 5, 8), (1, 1, 4, 4), (2, -1, 6, -4)):
        arrived(rs.at[buf], rs_s.at[buf], rs_r.at[buf])
        rs[buf] = rs[buf] + part[shard_of(shift)]
        go(rs.at[buf], rs.at[dst], rs_s.at[dst], rs_r.at[dst], device(dz=dz))
    arrived(low.at[3], low_s.at[3], low_r.at[3])
    for dx in (1, 2, 3):
        pl.when(x + dx >= XN)(to_row(dx, low.at[3]).start)
    for buf in (3, 4, 6, 5):
        arrived(rs.at[buf], rs_s.at[buf], rs_r.at[buf])
    total = (rs[3] + rs[4] + rs[5] + rs[6] + part[zb]) * (E ** -0.5)

    ft = (zb // 4 + xh) % 2
    row16 = 4 * zc + x
    c_rows = c_ref[row16 // 8, pl.ds(pl.multiple_of((row16 % 8) * 16, 16), 16),
                   pl.ds(pl.multiple_of((zb % 4) * 128, 128), 128)]
    sh, sl = split((B ** -0.5) * c_rows * total)
    shard[0] = sh
    shard[1] = sl
    xt = 2 * ft + core
    slot_n = nblk.at[rep, zc, zb, xl]
    own = jnp.logical_and(xt == x, core == rep)
    self_copy = pltpu.make_async_copy(shard, slot_n, m_r.at[0, xl])
    same_copy = remote(shard, slot_n, m_s.at[0, 0], m_r.at[0, xl], device(x_=xt, core_=rep))
    shifts = (0, 1, -1, 2, -2)
    for m in (3, 4, 1, 2):
        for other in range(2):
            go(shard, slot_n, m_s.at[m, other], m_r.at[m, xl],
               device(dz=4 * shifts[m], x_=xt, core_=rep, rep_=(rep + other) % 2))
    pl.when(own)(self_copy.start)
    pl.when(jnp.logical_not(own))(same_copy.start)
    go(shard, slot_n, m_s.at[0, 1], m_r.at[0, xl], device(x_=xt, core_=rep, rep_=1 - rep))

    dirs = (1, -1, 2)

    def to_window(block, index):
        for di, dz in enumerate(dirs):
            go(block, block, b_s.at[di, index], b_r.at[di, index], device(dz=dz))

    def own_block(shift):
        return nblk.at[core, zc, shard_of(-shift)]

    for m in range(5):
        block = own_block(shifts[m])
        for xs in range(2):
            arrived(nblk.at[core, zc, shard_of(-shifts[m]), xs], m_s.at[m, 0], m_r.at[m, xs])
        if shifts[m] == 2:
            go(block, block, f_s.at[1], f_r.at[1], device(dz=8))
            go(block, block, f_s.at[0], f_r.at[0], device(dz=4))
        if shifts[m] == -2:
            go(block, block, f_s.at[2], f_r.at[2], device(dz=-4))
        to_window(block, m)
    far = (3, -3, 4)
    for n, (shift, sem) in enumerate(((3, 0), (-3, 2), (4, 1))):
        block = own_block(shift)
        arrived(block, f_s.at[sem], f_r.at[sem])
        to_window(block, 5 + n)
    sibling = device(core_=1 - core)
    go(nblk.at[core, zc], nblk.at[core, zc], sib_s.at[0], sib_r.at[0], sibling)
    for di, dz in enumerate(dirs):
        zs = (z - dz + ZN) % ZN
        ks, js = zs // 4, zs % 4
        for index, shift in enumerate(shifts + far):
            kk = (ks - shift + 8) % 8
            arrived(nblk.at[core, js, kk], b_s.at[di, index], b_r.at[di, index])
        go(nblk.at[core, js], nblk.at[core, js], sib_s.at[1 + di], sib_r.at[1 + di], sibling)
    for n, dz in enumerate((0,) + dirs):
        js = (z - dz + ZN) % 4
        arrived(nblk.at[1 - core, js], sib_s.at[n], sib_r.at[n])

    def assemble(n, _):
        for p in range(2):
            for xs in range(2):
                for cb in range(4):
                    kk = 4 * ((xh + p) % 2) + cb
                    rows = pl.ds(pl.multiple_of(n * 64 + 32 * p + 16 * xs, 16), 16)
                    nhi[rows, 128 * cb:128 * cb + 128] = nblk[n // 4, n % 4, kk, xs, 0]
                    nlo[rows, 128 * cb:128 * cb + 128] = nblk[n // 4, n % 4, kk, xs, 1]
        return 0

    lax.fori_loop(0, 8, assemble, 0)

    arrived(csib, cs_s.at[0], cs_r.at[0])
    local = xl == core
    cw = jnp.where(local, c_ref[core], csib[...])
    count = ssteps_ref[xh]
    u1 = product(cw, nhi[...], nlo[...])
    u2 = product(u1, nhi[...], nlo[...])
    u3 = product(u2, nhi[...], nlo[...])
    w1 = cw - u1
    w2 = w1 + (u2 - u3)
    wown[...] = jnp.where(count >= 2, w2, jnp.where(count >= 1, w1, cw)).astype(BF16)
    slot_w = wbuf.at[xh, core]
    w_self = pltpu.make_async_copy(wown, slot_w, w_r.at[xh, core])
    w_sib = remote(wown, slot_w, w_s.at[0], w_r.at[xh, core], device(core_=xl))
    for dx in (1, 3, 2):
        go(wown, slot_w, w_s.at[dx], w_r.at[xh, core], device(dx=dx, core_=xl))
    pl.when(local)(w_self.start)
    pl.when(jnp.logical_not(local))(w_sib.start)

    for d in range(3):
        arrived(low.at[d], low_s.at[d], low_r.at[d])
    for n in range(2):
        arrived(con.at[n], con_s.at[n], con_r.at[n])
    for f in range(2):
        for half in range(2):
            arrived(wbuf.at[f, half], w_s.at[0], w_r.at[f, half])

    load_h.wait()
    scale = B ** -0.5
    valid = [jnp.where(energy >= offs[f], scale, 0.0).astype(F32) for f in range(2)]
    inside = jnp.where(jnp.logical_or(slab == 0, slab == 3), 0.0, 0.5 * scale).astype(F32)
    level = level_ref[0]
    lane = lax.broadcasted_iota(jnp.int32, (32, B), 1)
    line = lax.broadcasted_iota(jnp.int32, (32, B), 0) + rep * H

    def operator(n, carry):
        pair = pl.ds(2 * n, 2)
        rows = pl.ds(pl.multiple_of(n * 32, 32), 32)
        half_rows = pl.ds(pl.multiple_of((n % 4) * 32, 32), 32)
        diag = lane == line + n * 32
        self_energy = jnp.zeros((32, B), F32)
        for f in range(2):
            lw = low[offs[f] - 1, pair].reshape(32, B).astype(F32)
            wf = wbuf[f, n // 4, half_rows, :].astype(F32)
            self_energy = self_energy + lw * wf * valid[f]
        contact = (con[0, pair].reshape(32, B).astype(F32) * (0.5 * scale)
                   + con[1, pair].reshape(32, B).astype(F32) * inside)
        dyson = jnp.where(diag, level, 0.0) + h_ref[rows, :] - self_energy - contact
        dd = jnp.sum(jnp.where(diag, dyson, 0.0), axis=1, keepdims=True)
        iv = 1.0 / dd
        kk = jnp.where(diag, 0.0, dyson * iv)
        kf[rows, :] = kk
        kh, kl = split(kk)
        kbuf[rep, 0, rows, :] = kh
        kbuf[rep, 1, rows, :] = kl
        return carry + jnp.sum(jnp.where(diag, iv, 0.0), axis=0, keepdims=True)

    inv_row = lax.fori_loop(0, 8, operator, jnp.zeros((1, B), F32))
    inv[0] = jnp.broadcast_to(inv_row, (8, B))
    partner = device(rep_=1 - rep)
    go(kbuf.at[rep], kbuf.at[rep], k_s.at[0], k_r.at[0], partner)
    go(inv.at[0], inv.at[1], i_s.at[0], i_r.at[0], partner)
    for f in range(2):
        for half in range(2):
            w_ref[f, 128 * half:128 * half + 128, :] = wbuf[f, half]

    def columns(r):
        return pl.ds(pl.multiple_of(r * H, H), H)

    def partial(r):
        return product(kf[:, columns(r)], kbuf[r, 0], kbuf[r, 1])

    zbuf[...] = partial(rep)
    arrived(kbuf.at[1 - rep], k_s.at[0], k_r.at[0])
    arrived(inv.at[1], i_s.at[0], i_r.at[0])
    zbuf[...] = zbuf[...] + partial(1 - rep)
    cube = (product(zbuf[:, 0:H], kbuf[0, 0], kbuf[0, 1])
            + product(zbuf[:, H:B], kbuf[1, 0], kbuf[1, 1]))
    inv_all = inv[0][0:1, :] + inv[1][0:1, :]
    twice = gsteps_ref[0] >= 2
    full_lane = lax.broadcasted_iota(jnp.int32, (H, B), 1)
    full_line = lax.broadcasted_iota(jnp.int32, (H, B), 0) + rep * H
    ident = jnp.where(full_lane == full_line, 1.0, 0.0).astype(F32)
    first = ident - kf[...]
    out_ref[...] = jnp.where(twice, first + (zbuf[...] - cube), first) * inv_all

    for copy in pending:
        copy.wait_send()
    for dx in (1, 2, 3):
        to_row(dx, g_ref).wait_send()
    pl.when(jnp.logical_not(own))(same_copy.wait_send)
    pl.when(jnp.logical_not(local))(w_sib.wait_send)


def body(green_blocks, occupation, offsets, coulomb, hamiltonian, onsite_level, green_steps,
         screen_steps):
    smem = pl.BlockSpec(memory_space=pltpu.SMEM)
    hbm = pl.BlockSpec(memory_space=pl.ANY)
    vmem = pl.BlockSpec(memory_space=pltpu.VMEM)
    dma = pltpu.SemaphoreType.DMA
    sems = []
    for shape in ((5, 4), (5, 4), (4,), (2,), (1,), (7,), (5, 2), (3,), (3, 8), (4,)):
        sems += [dma(shape), dma(shape)]
    sems += [dma((4,)), dma((2, 2)), dma((1,)), dma((1,)), dma((1,)), dma((1,)), dma((3,)),
             pltpu.SemaphoreType.REGULAR]
    green, screened = pl.pallas_call(
        kernel,
        out_shape=(
            jax.ShapeDtypeStruct((H, B), F32),
            jax.ShapeDtypeStruct((2, H, B), BF16),
        ),
        in_specs=[smem] * 5 + [hbm] * 3,
        out_specs=(vmem, vmem),
        scratch_shapes=[
            pltpu.VMEM((16, 16, B), BF16),
            pltpu.VMEM((2, 128, B), F32),
            pltpu.VMEM((H, B), F32),
            pltpu.VMEM((20, 16, B), BF16),
            pltpu.VMEM((20, 8, 128), F32),
            pltpu.VMEM((4, 16, 16, B), BF16),
            pltpu.VMEM((2, 16, 16, B), BF16),
            pltpu.VMEM((128, B), F32),
            pltpu.VMEM((8, 16, 128), F32),
            pltpu.VMEM((7, 16, 128), F32),
            pltpu.VMEM((2, 16, 128), BF16),
            pltpu.VMEM((2, 4, 8, 2, 2, 16, 128), BF16),
            pltpu.VMEM((B, B), BF16),
            pltpu.VMEM((B, B), BF16),
            pltpu.VMEM((128, B), BF16),
            pltpu.VMEM((2, 2, 128, B), BF16),
            pltpu.VMEM((H, B), F32),
            pltpu.VMEM((2, 2, H, B), BF16),
            pltpu.VMEM((2, 8, B), F32),
            pltpu.VMEM((H, B), F32),
        ] + sems,
        compiler_params=pltpu.CompilerParams(
            collective_id=0, has_side_effects=True, vmem_limit_bytes=62 << 20
        ),
        name="gw_step",
    )(
        occupation, offsets, onsite_level, green_steps, screen_steps,
        green_blocks.reshape(16, 16, B), coulomb.reshape(2, 128, B), hamiltonian.reshape(H, B),
    )
    return green.reshape(1, 1, H, B), screened.reshape(2, 1, H, B)


def solution(mesh):
    return jax.shard_map(
        body,
        mesh=mesh,
        in_specs=(
            P("energy", "slab", "rep", None),
            P("energy"),
            P(),
            P("slab", "rep", None),
            P("slab", "rep", None),
            P("energy"),
            P("energy"),
            P(),
        ),
        out_specs=(P("energy", "slab", "rep", None), P(None, "slab", "rep", None)),
        check_vma=False,
    )
```

```python
import functools
import jax
import jax.numpy as jnp
from jax import lax
from jax.sharding import PartitionSpec as P
import jax.experimental.pallas as pl
import jax.experimental.pallas.tpu as pltpu

MESH = pl.DeviceIdType.MESH
B = 512
H = 256
XN = 4
ZN = 32
E = XN * ZN
F32 = jnp.float32
BF16 = jnp.bfloat16


def split(value):
    high = value.astype(BF16)
    low = (value - high.astype(F32)).astype(BF16)
    return high, low


def dot(a, b):
    return jnp.dot(a, b, preferred_element_type=F32)


def product(first, high, low):
    fh, fl = split(first)
    return dot(fh, high) + (dot(fh, low) + dot(fl, high))


def kernel(
    occ_ref, off_ref, level_ref, gsteps_ref, ssteps_ref, g_any, c_any, h_any,
    out_ref, w_ref,
    g_ref, c_ref, h_ref, gbuf, occbuf, low, con, cbuf, part, rs, shard, nblk, nhi, nlo, wown, wbuf,
    kf, kbuf, base, lsel, zbuf,
    p_s, p_r, o_s, o_r, low_s, low_r, con_s, con_r, cs_s, cs_r, rs_s, rs_r,
    m_s, m_r, f_s, f_r, b_s, b_r, sib_s, sib_r, w_s, w_r, e_s, e_r, in_s, tok,
):
    energy = lax.axis_index("energy")
    slab = lax.axis_index("slab")
    rep = lax.axis_index("rep")
    x, z = energy % XN, energy // XN
    yh, core = slab // 2, slab % 2
    zc, zb = z % 4, z // 4
    xh, xl = x // 2, x % 2

    def device(dx=0, dz=0, yh_=None, core_=None, rep_=None, x_=None):
        xx = (x + dx + XN) % XN if x_ is None else x_
        zz = (z + dz + ZN) % ZN
        yy = yh if yh_ is None else yh_
        cc = core if core_ is None else core_
        rr = rep if rep_ is None else rep_
        return (zz * XN + xx, yy * 2 + cc, rr)

    def remote(src, dst, send, recv, dev):
        return pltpu.make_async_remote_copy(
            src_ref=src, dst_ref=dst, send_sem=send, recv_sem=recv,
            device_id=dev, device_id_type=MESH,
        )

    def arrived(dst, send, recv):
        remote(dst, dst, send, recv, device(dx=1)).wait_recv()

    pending = []

    def go(*args):
        copy = remote(*args)
        copy.start()
        pending.append(copy)

    load_g = pltpu.make_async_copy(g_any, g_ref, in_s.at[0])
    load_c = pltpu.make_async_copy(c_any, c_ref, in_s.at[1])
    load_h = pltpu.make_async_copy(h_any, h_ref, in_s.at[2])
    load_g.start()

    barrier = pltpu.get_barrier_semaphore()
    peers = [
        device(dx=dx, core_=(core + dc) % 2, rep_=(rep + dr) % 2)
        for dx in range(4) for dc in range(2) for dr in range(2) if (dx, dc, dr) != (0, 0, 0)
    ]
    peers += [device(dx=dx, dz=dz) for dz in (1, -1, 2, -2) for dx in range(4)]
    peers += [device(dz=4), device(dz=-4), device(yh_=1 - yh, core_=1 - core)]
    for dev in peers:
        pl.semaphore_signal(barrier, inc=1, device_id=dev, device_id_type=MESH)
    occbuf[0] = jnp.full((8, 128), occ_ref[0], F32)
    load_c.start()
    load_h.start()
    load_g.wait()
    pl.semaphore_wait(barrier, len(peers))
    for dz in (4, -4):
        pl.semaphore_signal(tok, inc=1, device_id=device(dz=dz), device_id_type=MESH)

    for slot in (0, 4, 1, 3, 2):
        dz = 2 - slot
        for dx in range(4):
            if dz == 0 and dx == 0:
                continue
            xd = (x + dx) % XN
            row = 4 * ((z + dz + ZN) % 4) + xd
            go(g_ref.at[row], gbuf.at[slot * 4 + x], p_s.at[slot, dx], p_r.at[slot, dx],
               device(dx=dx, dz=dz))
            if slot > 0:
                go(occbuf.at[0], occbuf.at[slot * 4 + x], o_s.at[slot, dx], o_r.at[slot, dx],
                   device(dx=dx, dz=dz))
    go(g_ref, low.at[3], low_s.at[3], low_r.at[3], device(dz=1))
    gbuf[8 + x] = g_ref[4 * zc + x]
    occbuf[8 + x] = jnp.full((8, 128), occ_ref[0], F32)
    go(g_ref, con.at[0], con_s.at[0], con_r.at[0], device(core_=1 - core))
    go(g_ref, con.at[1], con_s.at[1], con_r.at[1], device(yh_=1 - yh, core_=1 - core))
    load_c.wait()
    holds = core == xl
    c_self = pltpu.make_async_copy(c_ref, cbuf, cs_r.at[0])
    c_same = remote(c_ref, cbuf, cs_s.at[0], cs_r.at[0], device(core_=rep))
    c_other = remote(c_ref, cbuf, cs_s.at[1], cs_r.at[0], device(core_=rep, rep_=1 - rep))
    c_here = jnp.logical_and(holds, core == rep)
    c_there = jnp.logical_and(holds, core != rep)
    pl.when(c_here)(c_self.start)
    pl.when(c_there)(c_same.start)
    pl.when(holds)(c_other.start)

    for slot in range(5):
        for dx in range(4):
            if slot == 2 and dx == 0:
                continue
            src_x = (x - dx + XN) % XN
            arrived(gbuf.at[slot * 4 + src_x], p_s.at[slot, dx], p_r.at[slot, dx])
            if slot > 0:
                arrived(occbuf.at[slot * 4 + src_x], o_s.at[slot, dx], o_r.at[slot, dx])

    offs = [jnp.clip(off_ref[f], 1, 4) for f in range(2)]

    def add_energy(n, carry):
        ee = 4 * ((z + n // 4 - 2 + ZN) % ZN) + n % 4
        cur = gbuf[n].astype(F32) * occbuf[n][0:1, 0:1]
        res = []
        for f in range(2):
            lowered = gbuf[n - offs[f]].astype(F32)
            valid = jnp.where(ee >= offs[f], 1.0, 0.0).astype(F32)
            res.append(carry[f] + cur * (lowered * valid))
        return tuple(res)

    zero = jnp.zeros((16, B), F32)
    acc = lax.fori_loop(4, 20, add_energy, (zero, zero))
    for f in range(2):
        for cb in range(4):
            part[4 * ((f + xh) % 2) + cb] = acc[f][:, 128 * cb:128 * cb + 128]

    def shard_of(shift):
        return (zb + shift + 8) % 8

    pl.semaphore_wait(tok, 2)
    go(part.at[shard_of(4)], rs.at[0], rs_s.at[0], rs_r.at[0], device(dz=8))
    go(part.at[shard_of(3)], rs.at[1], rs_s.at[1], rs_r.at[1], device(dz=8))
    go(part.at[shard_of(-3)], rs.at[2], rs_s.at[2], rs_r.at[2], device(dz=-8))
    go(part.at[shard_of(-2)], rs.at[3], rs_s.at[3], rs_r.at[3], device(dz=-8))

    def to_row(dx, src):
        return remote(src, low.at[dx - 1], low_s.at[dx - 1], low_r.at[dx - 1], device(dx=dx))

    for dx in (1, 2, 3):
        pl.when(x + dx < XN)(to_row(dx, g_ref).start)

    for n in range(2):
        arrived(con.at[n], con_s.at[n], con_r.at[n])
    load_h.wait()
    scale = B ** -0.5
    inside = jnp.where(jnp.logical_or(slab == 0, slab == 3), 0.0, 0.5 * scale).astype(F32)
    level = level_ref[0]
    lane = lax.broadcasted_iota(jnp.int32, (32, B), 1)
    line = lax.broadcasted_iota(jnp.int32, (32, B), 0)
    partner = device(rep_=1 - rep)

    def base_rows(n, _):
        pair = pl.ds(2 * n, 2)
        rows = pl.ds(pl.multiple_of(n * 32, 32), 32)
        contact = (con[0, pair].reshape(32, B).astype(F32) * (0.5 * scale)
                   + con[1, pair].reshape(32, B).astype(F32) * inside)
        diag = lane == line + (rep * H + n * 32)
        base[rep, rows, :] = jnp.where(diag, level, 0.0) + h_ref[rows, :] - contact
        return 0

    lax.fori_loop(0, 8, base_rows, 0)
    go(base.at[rep], base.at[rep], e_s.at[0], e_r.at[0], partner)

    for buf, shift, dst, dz in ((0, 2, 5, 8), (1, 1, 4, 4), (2, -1, 6, -4)):
        arrived(rs.at[buf], rs_s.at[buf], rs_r.at[buf])
        rs[buf] = rs[buf] + part[shard_of(shift)]
        go(rs.at[buf], rs.at[dst], rs_s.at[dst], rs_r.at[dst], device(dz=dz))
    arrived(low.at[3], low_s.at[3], low_r.at[3])
    for dx in (1, 2, 3):
        pl.when(x + dx >= XN)(to_row(dx, low.at[3]).start)
    for buf in (3, 4, 6, 5):
        arrived(rs.at[buf], rs_s.at[buf], rs_r.at[buf])
    total = (rs[3] + rs[4] + rs[5] + rs[6] + part[zb]) * (E ** -0.5)

    ft = (zb // 4 + xh) % 2
    row16 = 4 * zc + x
    c_rows = c_ref[row16 // 8, pl.ds(pl.multiple_of((row16 % 8) * 16, 16), 16),
                   pl.ds(pl.multiple_of((zb % 4) * 128, 128), 128)]
    sh, sl = split((B ** -0.5) * c_rows * total)
    shard[0] = sh
    shard[1] = sl
    xt = 2 * ft + core
    slot_n = nblk.at[rep, zc, zb, xl]
    own = jnp.logical_and(xt == x, core == rep)
    self_copy = pltpu.make_async_copy(shard, slot_n, m_r.at[0, xl])
    same_copy = remote(shard, slot_n, m_s.at[0, 0], m_r.at[0, xl], device(x_=xt, core_=rep))
    shifts = (0, 1, -1, 2, -2)
    for m in (3, 4, 1, 2):
        for other in range(2):
            go(shard, slot_n, m_s.at[m, other], m_r.at[m, xl],
               device(dz=4 * shifts[m], x_=xt, core_=rep, rep_=(rep + other) % 2))
    pl.when(own)(self_copy.start)
    pl.when(jnp.logical_not(own))(same_copy.start)
    go(shard, slot_n, m_s.at[0, 1], m_r.at[0, xl], device(x_=xt, core_=rep, rep_=1 - rep))

    dirs = (1, -1, 2)

    def to_window(block, index):
        for di, dz in enumerate(dirs):
            go(block, block, b_s.at[di, index], b_r.at[di, index], device(dz=dz))

    def own_block(shift):
        return nblk.at[core, zc, shard_of(-shift)]

    for m in range(5):
        block = own_block(shifts[m])
        for xs in range(2):
            arrived(nblk.at[core, zc, shard_of(-shifts[m]), xs], m_s.at[m, 0], m_r.at[m, xs])
        if shifts[m] == 2:
            go(block, block, f_s.at[1], f_r.at[1], device(dz=8))
            go(block, block, f_s.at[0], f_r.at[0], device(dz=4))
        if shifts[m] == -2:
            go(block, block, f_s.at[2], f_r.at[2], device(dz=-4))
        to_window(block, m)
    far = (3, -3, 4)
    for n, (shift, sem) in enumerate(((3, 0), (-3, 2), (4, 1))):
        block = own_block(shift)
        arrived(block, f_s.at[sem], f_r.at[sem])
        to_window(block, 5 + n)
    for d in range(3):
        arrived(low.at[d], low_s.at[d], low_r.at[d])

    def pick_rows(n, _):
        rows = pl.ds(pl.multiple_of(n * 32, 32), 32)
        for f in range(2):
            lw = low[offs[f] - 1, pl.ds(2 * n, 2)].reshape(32, B).astype(F32)
            lsel[rep, f, rows, :] = jnp.where(energy >= offs[f], lw, 0.0).astype(BF16)
        return 0

    sibling = device(core_=1 - core)
    go(nblk.at[core, zc], nblk.at[core, zc], sib_s.at[0], sib_r.at[0], sibling)
    lax.fori_loop(0, 8, pick_rows, 0)
    go(lsel.at[rep], lsel.at[rep], e_s.at[1], e_r.at[1], partner)
    for di, dz in enumerate(dirs):
        zs = (z - dz + ZN) % ZN
        ks, js = zs // 4, zs % 4
        for index, shift in enumerate(shifts + far):
            kk = (ks - shift + 8) % 8
            arrived(nblk.at[core, js, kk], b_s.at[di, index], b_r.at[di, index])
        go(nblk.at[core, js], nblk.at[core, js], sib_s.at[1 + di], sib_r.at[1 + di], sibling)
    for n, dz in enumerate((0,) + dirs):
        js = (z - dz + ZN) % 4
        arrived(nblk.at[1 - core, js], sib_s.at[n], sib_r.at[n])

    def assemble(n, _):
        for p in range(2):
            for xs in range(2):
                for cb in range(4):
                    kk = 4 * ((xh + p) % 2) + cb
                    rows = pl.ds(pl.multiple_of(n * 64 + 32 * p + 16 * xs, 16), 16)
                    nhi[rows, 128 * cb:128 * cb + 128] = nblk[n // 4, n % 4, kk, xs, 0]
                    nlo[rows, 128 * cb:128 * cb + 128] = nblk[n // 4, n % 4, kk, xs, 1]
        return 0

    lax.fori_loop(0, 8, assemble, 0)

    arrived(cbuf, cs_s.at[0], cs_r.at[0])
    local = xl == core
    cw = cbuf[...].reshape(H, B)
    count = ssteps_ref[xh]
    u1 = product(cw, nhi[...], nlo[...])
    u2 = product(u1, nhi[...], nlo[...])
    u3 = product(u2, nhi[...], nlo[...])
    w1 = cw - u1
    w2 = w1 + (u2 - u3)
    wown[...] = jnp.where(count >= 2, w2, jnp.where(count >= 1, w1, cw)).astype(BF16)
    slot_w = wbuf.at[xh, core]
    w_self = pltpu.make_async_copy(wown, slot_w, w_r.at[xh, core])
    w_sib = remote(wown, slot_w, w_s.at[0], w_r.at[xh, core], device(core_=xl))
    for dx in (1, 3, 2):
        go(wown, slot_w, w_s.at[dx], w_r.at[xh, core], device(dx=dx, core_=xl))
    pl.when(local)(w_self.start)
    pl.when(jnp.logical_not(local))(w_sib.start)

    for n, buf in enumerate((base, lsel)):
        arrived(buf.at[1 - rep], e_s.at[n], e_r.at[n])
    for f in range(2):
        for half in range(2):
            arrived(wbuf.at[f, half], w_s.at[0], w_r.at[f, half])

    def operator(n, carry):
        r = n // 8
        rows = pl.ds(pl.multiple_of((n % 8) * 32, 32), 32)
        self_energy = (lsel[r, 0, rows, :].astype(F32) * wbuf[0, r, rows, :].astype(F32)
                       + lsel[r, 1, rows, :].astype(F32) * wbuf[1, r, rows, :].astype(F32)) * scale
        dyson = base[r, rows, :] - self_energy
        diag = lane == line + n * 32
        dd = jnp.sum(jnp.where(diag, dyson, 0.0), axis=1, keepdims=True)
        iv = 1.0 / dd
        kk = jnp.where(diag, 0.0, dyson * iv)
        kf[r, rows, :] = kk
        kh, kl = split(kk)
        kbuf[r, 0, rows, :] = kh
        kbuf[r, 1, rows, :] = kl
        return carry + jnp.sum(jnp.where(diag, iv, 0.0), axis=0, keepdims=True)

    inv_all = lax.fori_loop(0, 16, operator, jnp.zeros((1, B), F32))
    for f in range(2):
        w_ref[f] = wbuf[f, rep]

    zbuf[...] = (product(kf[rep, :, 0:H], kbuf[0, 0], kbuf[0, 1])
                 + product(kf[rep, :, H:B], kbuf[1, 0], kbuf[1, 1]))
    cube = (product(zbuf[:, 0:H], kbuf[0, 0], kbuf[0, 1])
            + product(zbuf[:, H:B], kbuf[1, 0], kbuf[1, 1]))
    twice = gsteps_ref[0] >= 2
    full_lane = lax.broadcasted_iota(jnp.int32, (H, B), 1)
    full_line = lax.broadcasted_iota(jnp.int32, (H, B), 0) + rep * H
    ident = jnp.where(full_lane == full_line, 1.0, 0.0).astype(F32)
    first = ident - kf[rep]
    out_ref[...] = jnp.where(twice, first + (zbuf[...] - cube), first) * inv_all

    for copy in pending:
        copy.wait_send()
    for dx in (1, 2, 3):
        to_row(dx, g_ref).wait_send()
    pl.when(jnp.logical_not(own))(same_copy.wait_send)
    pl.when(jnp.logical_not(local))(w_sib.wait_send)
    pl.when(c_there)(c_same.wait_send)
    pl.when(holds)(c_other.wait_send)


def body(green_blocks, occupation, offsets, coulomb, hamiltonian, onsite_level, green_steps,
         screen_steps):
    smem = pl.BlockSpec(memory_space=pltpu.SMEM)
    hbm = pl.BlockSpec(memory_space=pl.ANY)
    vmem = pl.BlockSpec(memory_space=pltpu.VMEM)
    dma = pltpu.SemaphoreType.DMA
    sems = []
    for shape in ((5, 4), (5, 4), (4,), (2,), (2,), (7,), (5, 2), (3,), (3, 8), (4,)):
        sems += [dma(shape), dma(shape)]
    sems += [dma((4,)), dma((2, 2)), dma((2,)), dma((2,)), dma((3,)),
             pltpu.SemaphoreType.REGULAR]
    green, screened = pl.pallas_call(
        kernel,
        out_shape=(
            jax.ShapeDtypeStruct((H, B), F32),
            jax.ShapeDtypeStruct((2, H, B), BF16),
        ),
        in_specs=[smem] * 5 + [hbm] * 3,
        out_specs=(vmem, vmem),
        scratch_shapes=[
            pltpu.VMEM((16, 16, B), BF16),
            pltpu.VMEM((2, 128, B), F32),
            pltpu.VMEM((H, B), F32),
            pltpu.VMEM((20, 16, B), BF16),
            pltpu.VMEM((20, 8, 128), F32),
            pltpu.VMEM((4, 16, 16, B), BF16),
            pltpu.VMEM((2, 16, 16, B), BF16),
            pltpu.VMEM((2, 128, B), F32),
            pltpu.VMEM((8, 16, 128), F32),
            pltpu.VMEM((7, 16, 128), F32),
            pltpu.VMEM((2, 16, 128), BF16),
            pltpu.VMEM((2, 4, 8, 2, 2, 16, 128), BF16),
            pltpu.VMEM((B, B), BF16),
            pltpu.VMEM((B, B), BF16),
            pltpu.VMEM((H, B), BF16),
            pltpu.VMEM((2, 2, H, B), BF16),
            pltpu.VMEM((2, H, B), F32),
            pltpu.VMEM((2, 2, H, B), BF16),
            pltpu.VMEM((2, H, B), F32),
            pltpu.VMEM((2, 2, H, B), BF16),
            pltpu.VMEM((H, B), F32),
        ] + sems,
        compiler_params=pltpu.CompilerParams(
            collective_id=0, has_side_effects=True, vmem_limit_bytes=62 << 20
        ),
        name="gw_step",
    )(
        occupation, offsets, onsite_level, green_steps, screen_steps,
        green_blocks.reshape(16, 16, B), coulomb.reshape(2, 128, B), hamiltonian.reshape(H, B),
    )
    return green.reshape(1, 1, H, B), screened.reshape(2, 1, H, B)


def solution(mesh):
    return jax.shard_map(
        body,
        mesh=mesh,
        in_specs=(
            P("energy", "slab", "rep", None),
            P("energy"),
            P(),
            P("slab", "rep", None),
            P("slab", "rep", None),
            P("energy"),
            P("energy"),
            P(),
        ),
        out_specs=(P("energy", "slab", "rep", None), P(None, "slab", "rep", None)),
        check_vma=False,
    )
```

```python
import functools
import jax
import jax.numpy as jnp
from jax import lax
from jax.sharding import PartitionSpec as P
import jax.experimental.pallas as pl
import jax.experimental.pallas.tpu as pltpu

MESH = pl.DeviceIdType.MESH
B = 512
H = 256
XN = 4
ZN = 32
E = XN * ZN
F32 = jnp.float32
BF16 = jnp.bfloat16


def split(value):
    high = value.astype(BF16)
    low = (value - high.astype(F32)).astype(BF16)
    return high, low


def dot(a, b):
    return jnp.dot(a, b, preferred_element_type=F32)


def product(first, high, low):
    fh, fl = split(first)
    return dot(fh, high) + (dot(fh, low) + dot(fl, high))


def kernel(
    occ_ref, off_ref, level_ref, gsteps_ref, ssteps_ref, g_any, c_any, h_any,
    out_ref, w_ref,
    g_ref, c_ref, h_ref, gbuf, occbuf, low, con, cbuf, part, rs, shard, nblk, nhi, nlo, wown, wbuf,
    kf, kbuf, base, lsel, zbuf,
    p_s, p_r, o_s, o_r, low_s, low_r, con_s, con_r, cs_s, cs_r, rs_s, rs_r,
    m_s, m_r, f_s, f_r, b_s, b_r, sib_s, sib_r, w_s, w_r, e_s, e_r, in_s, tok,
):
    energy = lax.axis_index("energy")
    slab = lax.axis_index("slab")
    rep = lax.axis_index("rep")
    x, z = energy % XN, energy // XN
    yh, core = slab // 2, slab % 2
    zc, zb = z % 4, z // 4
    xh, xl = x // 2, x % 2

    def device(dx=0, dz=0, yh_=None, core_=None, rep_=None, x_=None):
        xx = (x + dx + XN) % XN if x_ is None else x_
        zz = (z + dz + ZN) % ZN
        yy = yh if yh_ is None else yh_
        cc = core if core_ is None else core_
        rr = rep if rep_ is None else rep_
        return (zz * XN + xx, yy * 2 + cc, rr)

    def remote(src, dst, send, recv, dev):
        return pltpu.make_async_remote_copy(
            src_ref=src, dst_ref=dst, send_sem=send, recv_sem=recv,
            device_id=dev, device_id_type=MESH,
        )

    def arrived(dst, send, recv):
        remote(dst, dst, send, recv, device(dx=1)).wait_recv()

    pending = []

    def go(*args):
        copy = remote(*args)
        copy.start()
        pending.append(copy)

    load_g = pltpu.make_async_copy(g_any, g_ref, in_s.at[0])
    load_c = pltpu.make_async_copy(c_any, c_ref, in_s.at[1])
    load_h = pltpu.make_async_copy(h_any, h_ref, in_s.at[2])
    load_g.start()

    barrier = pltpu.get_barrier_semaphore()
    peers = [
        device(dx=dx, core_=(core + dc) % 2, rep_=(rep + dr) % 2)
        for dx in range(4) for dc in range(2) for dr in range(2) if (dx, dc, dr) != (0, 0, 0)
    ]
    peers += [device(dx=dx, dz=dz) for dz in (1, -1, 2, -2) for dx in range(4)]
    peers += [device(dz=4), device(dz=-4), device(yh_=1 - yh, core_=1 - core)]
    for dev in peers:
        pl.semaphore_signal(barrier, inc=1, device_id=dev, device_id_type=MESH)
    occbuf[0] = jnp.full((8, 128), occ_ref[0], F32)
    load_c.start()
    load_h.start()
    load_g.wait()
    pl.semaphore_wait(barrier, len(peers))
    for dz in (4, -4):
        pl.semaphore_signal(tok, inc=1, device_id=device(dz=dz), device_id_type=MESH)

    for slot in (0, 4, 1, 3, 2):
        dz = 2 - slot
        for dx in range(4):
            if dz == 0 and dx == 0:
                continue
            xd = (x + dx) % XN
            row = 4 * ((z + dz + ZN) % 4) + xd
            go(g_ref.at[row], gbuf.at[slot * 4 + x], p_s.at[slot, dx], p_r.at[slot, dx],
               device(dx=dx, dz=dz))
            if slot > 0:
                go(occbuf.at[0], occbuf.at[slot * 4 + x], o_s.at[slot, dx], o_r.at[slot, dx],
                   device(dx=dx, dz=dz))
    go(g_ref, low.at[3], low_s.at[3], low_r.at[3], device(dz=1))
    gbuf[8 + x] = g_ref[4 * zc + x]
    occbuf[8 + x] = jnp.full((8, 128), occ_ref[0], F32)
    go(g_ref, con.at[0], con_s.at[0], con_r.at[0], device(core_=1 - core))
    go(g_ref, con.at[1], con_s.at[1], con_r.at[1], device(yh_=1 - yh, core_=1 - core))
    load_c.wait()
    holds = core == xl
    c_self = pltpu.make_async_copy(c_ref, cbuf, cs_r.at[0])
    c_same = remote(c_ref, cbuf, cs_s.at[0], cs_r.at[0], device(core_=rep))
    c_other = remote(c_ref, cbuf, cs_s.at[1], cs_r.at[0], device(core_=rep, rep_=1 - rep))
    c_here = jnp.logical_and(holds, core == rep)
    c_there = jnp.logical_and(holds, core != rep)
    pl.when(c_here)(c_self.start)
    pl.when(c_there)(c_same.start)
    pl.when(holds)(c_other.start)

    for slot in range(5):
        for dx in range(4):
            if slot == 2 and dx == 0:
                continue
            src_x = (x - dx + XN) % XN
            arrived(gbuf.at[slot * 4 + src_x], p_s.at[slot, dx], p_r.at[slot, dx])
            if slot > 0:
                arrived(occbuf.at[slot * 4 + src_x], o_s.at[slot, dx], o_r.at[slot, dx])

    offs = [jnp.clip(off_ref[f], 1, 4) for f in range(2)]

    def add_energy(n, carry):
        ee = 4 * ((z + n // 4 - 2 + ZN) % ZN) + n % 4
        cur = gbuf[n].astype(F32) * occbuf[n][0:1, 0:1]
        res = []
        for f in range(2):
            lowered = gbuf[n - offs[f]].astype(F32)
            valid = jnp.where(ee >= offs[f], 1.0, 0.0).astype(F32)
            res.append(carry[f] + cur * (lowered * valid))
        return tuple(res)

    zero = jnp.zeros((16, B), F32)
    acc = lax.fori_loop(4, 20, add_energy, (zero, zero))
    for f in range(2):
        for cb in range(4):
            part[4 * ((f + xh) % 2) + cb] = acc[f][:, 128 * cb:128 * cb + 128]

    def shard_of(shift):
        return (zb + shift + 8) % 8

    pl.semaphore_wait(tok, 2)
    go(part.at[shard_of(4)], rs.at[0], rs_s.at[0], rs_r.at[0], device(dz=8))
    go(part.at[shard_of(3)], rs.at[1], rs_s.at[1], rs_r.at[1], device(dz=8))
    go(part.at[shard_of(-3)], rs.at[2], rs_s.at[2], rs_r.at[2], device(dz=-8))
    go(part.at[shard_of(-2)], rs.at[3], rs_s.at[3], rs_r.at[3], device(dz=-8))

    def to_row(dx, src):
        return remote(src, low.at[dx - 1], low_s.at[dx - 1], low_r.at[dx - 1], device(dx=dx))

    for dx in (1, 2, 3):
        pl.when(x + dx < XN)(to_row(dx, g_ref).start)

    for n in range(2):
        arrived(con.at[n], con_s.at[n], con_r.at[n])
    load_h.wait()
    scale = B ** -0.5
    inside = jnp.where(jnp.logical_or(slab == 0, slab == 3), 0.0, 0.5 * scale).astype(F32)
    level = level_ref[0]
    lane = lax.broadcasted_iota(jnp.int32, (32, B), 1)
    line = lax.broadcasted_iota(jnp.int32, (32, B), 0)
    partner = device(rep_=1 - rep)

    def base_rows(n, _):
        pair = pl.ds(2 * n, 2)
        rows = pl.ds(pl.multiple_of(n * 32, 32), 32)
        contact = (con[0, pair].reshape(32, B).astype(F32) * (0.5 * scale)
                   + con[1, pair].reshape(32, B).astype(F32) * inside)
        diag = lane == line + (rep * H + n * 32)
        base[rep, rows, :] = jnp.where(diag, level, 0.0) + h_ref[rows, :] - contact
        return 0

    lax.fori_loop(0, 8, base_rows, 0)
    go(base.at[rep], base.at[rep], e_s.at[0], e_r.at[0], partner)

    for buf, shift, dst, dz in ((0, 2, 5, 8), (1, 1, 4, 4), (2, -1, 6, -4)):
        arrived(rs.at[buf], rs_s.at[buf], rs_r.at[buf])
        rs[buf] = rs[buf] + part[shard_of(shift)]
        go(rs.at[buf], rs.at[dst], rs_s.at[dst], rs_r.at[dst], device(dz=dz))
    arrived(low.at[3], low_s.at[3], low_r.at[3])
    for dx in (1, 2, 3):
        pl.when(x + dx >= XN)(to_row(dx, low.at[3]).start)
    for buf in (3, 4, 6, 5):
        arrived(rs.at[buf], rs_s.at[buf], rs_r.at[buf])
    total = (rs[3] + rs[4] + rs[5] + rs[6] + part[zb]) * (E ** -0.5)

    ft = (zb // 4 + xh) % 2
    row16 = 4 * zc + x
    c_rows = c_ref[row16 // 8, pl.ds(pl.multiple_of((row16 % 8) * 16, 16), 16),
                   pl.ds(pl.multiple_of((zb % 4) * 128, 128), 128)]
    sh, sl = split((B ** -0.5) * c_rows * total)
    shard[0] = sh
    shard[1] = sl
    fm = (xh + rep) % 2

    def column(rep_):
        return 2 * ((ft + rep_) % 2) + core

    xt = column(rep)
    slot_n = nblk.at[rep, zc, zb, xl]
    own = jnp.logical_and(xt == x, core == rep)
    self_copy = pltpu.make_async_copy(shard, slot_n, m_r.at[0, xl])
    same_copy = remote(shard, slot_n, m_s.at[0, 0], m_r.at[0, xl], device(x_=xt, core_=rep))
    shifts = (0, 1, -1, 2, -2)
    for m in (3, 4, 1, 2):
        for other in range(2):
            go(shard, slot_n, m_s.at[m, other], m_r.at[m, xl],
               device(dz=4 * shifts[m], x_=column((rep + other) % 2), core_=rep,
                      rep_=(rep + other) % 2))
    pl.when(own)(self_copy.start)
    pl.when(jnp.logical_not(own))(same_copy.start)
    go(shard, slot_n, m_s.at[0, 1], m_r.at[0, xl],
       device(x_=column(1 - rep), core_=rep, rep_=1 - rep))

    dirs = (1, -1, 2)

    def to_window(block, index):
        for di, dz in enumerate(dirs):
            go(block, block, b_s.at[di, index], b_r.at[di, index], device(dz=dz))

    def own_block(shift):
        return nblk.at[core, zc, shard_of(-shift)]

    for m in range(5):
        block = own_block(shifts[m])
        for xs in range(2):
            arrived(nblk.at[core, zc, shard_of(-shifts[m]), xs], m_s.at[m, 0], m_r.at[m, xs])
        if shifts[m] == 2:
            go(block, block, f_s.at[1], f_r.at[1], device(dz=8))
            go(block, block, f_s.at[0], f_r.at[0], device(dz=4))
        if shifts[m] == -2:
            go(block, block, f_s.at[2], f_r.at[2], device(dz=-4))
        to_window(block, m)
    for d in range(3):
        arrived(low.at[d], low_s.at[d], low_r.at[d])

    def pick_rows(n, _):
        rows = pl.ds(pl.multiple_of(n * 32, 32), 32)
        for f in range(2):
            lw = low[offs[f] - 1, pl.ds(2 * n, 2)].reshape(32, B).astype(F32)
            lsel[rep, f, rows, :] = jnp.where(energy >= offs[f], lw, 0.0).astype(BF16)
        return 0

    lax.fori_loop(0, 8, pick_rows, 0)
    go(lsel.at[rep], lsel.at[rep], e_s.at[1], e_r.at[1], partner)
    far = (3, -3, 4)
    for n, (shift, sem) in enumerate(((3, 0), (-3, 2), (4, 1))):
        block = own_block(shift)
        arrived(block, f_s.at[sem], f_r.at[sem])
        to_window(block, 5 + n)
    sibling = device(core_=1 - core)
    go(nblk.at[core, zc], nblk.at[core, zc], sib_s.at[0], sib_r.at[0], sibling)
    for di, dz in enumerate(dirs):
        zs = (z - dz + ZN) % ZN
        ks, js = zs // 4, zs % 4
        for index, shift in enumerate(shifts + far):
            kk = (ks - shift + 8) % 8
            arrived(nblk.at[core, js, kk], b_s.at[di, index], b_r.at[di, index])
        go(nblk.at[core, js], nblk.at[core, js], sib_s.at[1 + di], sib_r.at[1 + di], sibling)
    for n, dz in enumerate((0,) + dirs):
        js = (z - dz + ZN) % 4
        arrived(nblk.at[1 - core, js], sib_s.at[n], sib_r.at[n])

    def assemble(n, _):
        for p in range(2):
            for xs in range(2):
                for cb in range(4):
                    kk = 4 * ((fm + p) % 2) + cb
                    rows = pl.ds(pl.multiple_of(n * 64 + 32 * p + 16 * xs, 16), 16)
                    nhi[rows, 128 * cb:128 * cb + 128] = nblk[n // 4, n % 4, kk, xs, 0]
                    nlo[rows, 128 * cb:128 * cb + 128] = nblk[n // 4, n % 4, kk, xs, 1]
        return 0

    lax.fori_loop(0, 8, assemble, 0)

    arrived(cbuf, cs_s.at[0], cs_r.at[0])
    local = xl == core
    cw = cbuf[...].reshape(H, B)
    count = ssteps_ref[fm]
    u1 = product(cw, nhi[...], nlo[...])
    u2 = product(u1, nhi[...], nlo[...])
    u3 = product(u2, nhi[...], nlo[...])
    w1 = cw - u1
    w2 = w1 + (u2 - u3)
    wown[...] = jnp.where(count >= 2, w2, jnp.where(count >= 1, w1, cw)).astype(BF16)
    slot_w = wbuf.at[fm, core]
    w_self = pltpu.make_async_copy(wown, slot_w, w_r.at[fm, core])
    w_sib = remote(wown, slot_w, w_s.at[0], w_r.at[fm, core], device(core_=xl))
    for n, dev in enumerate((device(dx=1, core_=xl), device(dx=-1, core_=xl),
                             device(core_=xl, rep_=1 - rep))):
        go(wown, slot_w, w_s.at[1 + n], w_r.at[fm, core], dev)
    pl.when(local)(w_self.start)
    pl.when(jnp.logical_not(local))(w_sib.start)

    for n, buf in enumerate((base, lsel)):
        arrived(buf.at[1 - rep], e_s.at[n], e_r.at[n])
    for f in range(2):
        for half in range(2):
            arrived(wbuf.at[f, half], w_s.at[0], w_r.at[f, half])

    def operator(n, carry):
        r = n // 8
        rows = pl.ds(pl.multiple_of((n % 8) * 32, 32), 32)
        self_energy = (lsel[r, 0, rows, :].astype(F32) * wbuf[0, r, rows, :].astype(F32)
                       + lsel[r, 1, rows, :].astype(F32) * wbuf[1, r, rows, :].astype(F32)) * scale
        dyson = base[r, rows, :] - self_energy
        diag = lane == line + n * 32
        dd = jnp.sum(jnp.where(diag, dyson, 0.0), axis=1, keepdims=True)
        iv = 1.0 / dd
        kk = jnp.where(diag, 0.0, dyson * iv)
        kf[r, rows, :] = kk
        kh, kl = split(kk)
        kbuf[r, 0, rows, :] = kh
        kbuf[r, 1, rows, :] = kl
        return carry + jnp.sum(jnp.where(diag, iv, 0.0), axis=0, keepdims=True)

    inv_all = lax.fori_loop(0, 16, operator, jnp.zeros((1, B), F32))
    for f in range(2):
        w_ref[f] = wbuf[f, rep]

    zbuf[...] = (product(kf[rep, :, 0:H], kbuf[0, 0], kbuf[0, 1])
                 + product(kf[rep, :, H:B], kbuf[1, 0], kbuf[1, 1]))
    cube = (product(zbuf[:, 0:H], kbuf[0, 0], kbuf[0, 1])
            + product(zbuf[:, H:B], kbuf[1, 0], kbuf[1, 1]))
    twice = gsteps_ref[0] >= 2
    full_lane = lax.broadcasted_iota(jnp.int32, (H, B), 1)
    full_line = lax.broadcasted_iota(jnp.int32, (H, B), 0) + rep * H
    ident = jnp.where(full_lane == full_line, 1.0, 0.0).astype(F32)
    first = ident - kf[rep]
    out_ref[...] = jnp.where(twice, first + (zbuf[...] - cube), first) * inv_all

    for copy in pending:
        copy.wait_send()
    for dx in (1, 2, 3):
        to_row(dx, g_ref).wait_send()
    pl.when(jnp.logical_not(own))(same_copy.wait_send)
    pl.when(jnp.logical_not(local))(w_sib.wait_send)
    pl.when(c_there)(c_same.wait_send)
    pl.when(holds)(c_other.wait_send)


def body(green_blocks, occupation, offsets, coulomb, hamiltonian, onsite_level, green_steps,
         screen_steps):
    smem = pl.BlockSpec(memory_space=pltpu.SMEM)
    hbm = pl.BlockSpec(memory_space=pl.ANY)
    vmem = pl.BlockSpec(memory_space=pltpu.VMEM)
    dma = pltpu.SemaphoreType.DMA
    sems = []
    for shape in ((5, 4), (5, 4), (4,), (2,), (2,), (7,), (5, 2), (3,), (3, 8), (4,)):
        sems += [dma(shape), dma(shape)]
    sems += [dma((4,)), dma((2, 2)), dma((2,)), dma((2,)), dma((3,)),
             pltpu.SemaphoreType.REGULAR]
    green, screened = pl.pallas_call(
        kernel,
        out_shape=(
            jax.ShapeDtypeStruct((H, B), F32),
            jax.ShapeDtypeStruct((2, H, B), BF16),
        ),
        in_specs=[smem] * 5 + [hbm] * 3,
        out_specs=(vmem, vmem),
        scratch_shapes=[
            pltpu.VMEM((16, 16, B), BF16),
            pltpu.VMEM((2, 128, B), F32),
            pltpu.VMEM((H, B), F32),
            pltpu.VMEM((20, 16, B), BF16),
            pltpu.VMEM((20, 8, 128), F32),
            pltpu.VMEM((4, 16, 16, B), BF16),
            pltpu.VMEM((2, 16, 16, B), BF16),
            pltpu.VMEM((2, 128, B), F32),
            pltpu.VMEM((8, 16, 128), F32),
            pltpu.VMEM((7, 16, 128), F32),
            pltpu.VMEM((2, 16, 128), BF16),
            pltpu.VMEM((2, 4, 8, 2, 2, 16, 128), BF16),
            pltpu.VMEM((B, B), BF16),
            pltpu.VMEM((B, B), BF16),
            pltpu.VMEM((H, B), BF16),
            pltpu.VMEM((2, 2, H, B), BF16),
            pltpu.VMEM((2, H, B), F32),
            pltpu.VMEM((2, 2, H, B), BF16),
            pltpu.VMEM((2, H, B), F32),
            pltpu.VMEM((2, 2, H, B), BF16),
            pltpu.VMEM((H, B), F32),
        ] + sems,
        compiler_params=pltpu.CompilerParams(
            collective_id=0, has_side_effects=True, vmem_limit_bytes=62 << 20
        ),
        name="gw_step",
    )(
        occupation, offsets, onsite_level, green_steps, screen_steps,
        green_blocks.reshape(16, 16, B), coulomb.reshape(2, 128, B), hamiltonian.reshape(H, B),
    )
    return green.reshape(1, 1, H, B), screened.reshape(2, 1, H, B)


def solution(mesh):
    return jax.shard_map(
        body,
        mesh=mesh,
        in_specs=(
            P("energy", "slab", "rep", None),
            P("energy"),
            P(),
            P("slab", "rep", None),
            P("slab", "rep", None),
            P("energy"),
            P("energy"),
            P(),
        ),
        out_specs=(P("energy", "slab", "rep", None), P(None, "slab", "rep", None)),
        check_vma=False,
    )
```

```python
import functools
import jax
import jax.numpy as jnp
from jax import lax
from jax.sharding import PartitionSpec as P
import jax.experimental.pallas as pl
import jax.experimental.pallas.tpu as pltpu

MESH = pl.DeviceIdType.MESH
B = 512
H = 256
XN = 4
ZN = 32
E = XN * ZN
F32 = jnp.float32
BF16 = jnp.bfloat16


def split(value):
    high = value.astype(BF16)
    low = (value - high.astype(F32)).astype(BF16)
    return high, low


def dot(a, b):
    return jnp.dot(a, b, preferred_element_type=F32)


def product(first, high, low):
    fh, fl = split(first)
    return dot(fh, high) + (dot(fh, low) + dot(fl, high))


def kernel(
    occ_ref, off_ref, level_ref, gsteps_ref, ssteps_ref, g_any, c_any, h_any,
    out_ref, w_ref, inv_ref,
    g_ref, c_ref, h_ref, gbuf, occbuf, low, con, cbuf, part, rs, shard, nblk, nhi, nlo, wown, wbuf,
    kf, kbuf, base, lsel, zbuf,
    p_s, p_r, o_s, o_r, low_s, low_r, con_s, con_r, cs_s, cs_r, rs_s, rs_r,
    m_s, m_r, f_s, f_r, b_s, b_r, sib_s, sib_r, w_s, w_r, e_s, e_r, in_s, tok,
):
    energy = lax.axis_index("energy")
    slab = lax.axis_index("slab")
    rep = lax.axis_index("rep")
    x, z = energy % XN, energy // XN
    yh, core = slab // 2, slab % 2
    zc, zb = z % 4, z // 4
    xh, xl = x // 2, x % 2

    def device(dx=0, dz=0, yh_=None, core_=None, rep_=None, x_=None):
        xx = (x + dx + XN) % XN if x_ is None else x_
        zz = (z + dz + ZN) % ZN
        yy = yh if yh_ is None else yh_
        cc = core if core_ is None else core_
        rr = rep if rep_ is None else rep_
        return (zz * XN + xx, yy * 2 + cc, rr)

    def remote(src, dst, send, recv, dev):
        return pltpu.make_async_remote_copy(
            src_ref=src, dst_ref=dst, send_sem=send, recv_sem=recv,
            device_id=dev, device_id_type=MESH,
        )

    def arrived(dst, send, recv):
        remote(dst, dst, send, recv, device(dx=1)).wait_recv()

    pending = []

    def go(*args):
        copy = remote(*args)
        copy.start()
        pending.append(copy)

    load_g = pltpu.make_async_copy(g_any, g_ref, in_s.at[0])
    load_c = pltpu.make_async_copy(c_any, c_ref, in_s.at[1])
    load_h = pltpu.make_async_copy(h_any, h_ref, in_s.at[2])
    load_g.start()

    barrier = pltpu.get_barrier_semaphore()
    peers = [
        device(dx=dx, core_=(core + dc) % 2, rep_=(rep + dr) % 2)
        for dx in range(4) for dc in range(2) for dr in range(2) if (dx, dc, dr) != (0, 0, 0)
    ]
    peers += [device(dx=dx, dz=dz) for dz in (1, -1, 2, -2) for dx in range(4)]
    peers += [device(dz=4), device(dz=-4), device(yh_=1 - yh, core_=1 - core)]
    for dev in peers:
        pl.semaphore_signal(barrier, inc=1, device_id=dev, device_id_type=MESH)
    occbuf[0] = jnp.full((8, 128), occ_ref[0], F32)
    load_c.start()
    load_h.start()
    load_g.wait()
    pl.semaphore_wait(barrier, len(peers))
    for dz in (4, -4):
        pl.semaphore_signal(tok, inc=1, device_id=device(dz=dz), device_id_type=MESH)

    for slot in (0, 4, 1, 3, 2):
        dz = 2 - slot
        for dx in range(4):
            if dz == 0 and dx == 0:
                continue
            xd = (x + dx) % XN
            row = 4 * ((z + dz + ZN) % 4) + xd
            go(g_ref.at[row], gbuf.at[slot * 4 + x], p_s.at[slot, dx], p_r.at[slot, dx],
               device(dx=dx, dz=dz))
            if slot > 0:
                go(occbuf.at[0], occbuf.at[slot * 4 + x], o_s.at[slot, dx], o_r.at[slot, dx],
                   device(dx=dx, dz=dz))
    gbuf[8 + x] = g_ref[4 * zc + x]
    occbuf[8 + x] = jnp.full((8, 128), occ_ref[0], F32)
    go(g_ref, con.at[0], con_s.at[0], con_r.at[0], device(core_=1 - core))
    edge = jnp.logical_or(slab == 0, slab == 3)
    beside = remote(g_ref, con.at[1], con_s.at[1], con_r.at[1],
                    device(yh_=1 - yh, core_=1 - core))
    pl.when(jnp.logical_not(edge))(beside.start)

    @pl.when(edge)
    def _():
        con[1] = jnp.zeros((16, 16, B), BF16)

    load_c.wait()
    holds = core == xl
    c_self = pltpu.make_async_copy(c_ref, cbuf, cs_r.at[0])
    c_same = remote(c_ref, cbuf, cs_s.at[0], cs_r.at[0], device(core_=rep))
    c_other = remote(c_ref, cbuf, cs_s.at[1], cs_r.at[0], device(core_=rep, rep_=1 - rep))
    c_here = jnp.logical_and(holds, core == rep)
    c_there = jnp.logical_and(holds, core != rep)
    pl.when(c_here)(c_self.start)
    pl.when(c_there)(c_same.start)
    pl.when(holds)(c_other.start)

    for slot in range(5):
        for dx in range(4):
            if slot == 2 and dx == 0:
                continue
            src_x = (x - dx + XN) % XN
            arrived(gbuf.at[slot * 4 + src_x], p_s.at[slot, dx], p_r.at[slot, dx])
            if slot > 0:
                arrived(occbuf.at[slot * 4 + src_x], o_s.at[slot, dx], o_r.at[slot, dx])

    offs = [jnp.clip(off_ref[f], 1, 4) for f in range(2)]

    def add_energy(n, carry):
        ee = 4 * ((z + n // 4 - 2 + ZN) % ZN) + n % 4
        cur = gbuf[n].astype(F32) * occbuf[n][0:1, 0:1]
        res = []
        for f in range(2):
            lowered = gbuf[n - offs[f]].astype(F32)
            valid = jnp.where(ee >= offs[f], 1.0, 0.0).astype(F32)
            res.append(carry[f] + cur * (lowered * valid))
        return tuple(res)

    zero = jnp.zeros((16, B), F32)
    acc = lax.fori_loop(4, 20, add_energy, (zero, zero))
    for f in range(2):
        for cb in range(4):
            part[4 * ((f + xh) % 2) + cb] = acc[f][:, 128 * cb:128 * cb + 128]

    def shard_of(shift):
        return (zb + shift + 8) % 8

    pl.semaphore_wait(tok, 2)
    go(part.at[shard_of(4)], rs.at[0], rs_s.at[0], rs_r.at[0], device(dz=8))
    go(part.at[shard_of(3)], rs.at[1], rs_s.at[1], rs_r.at[1], device(dz=8))
    go(part.at[shard_of(-3)], rs.at[2], rs_s.at[2], rs_r.at[2], device(dz=-8))
    go(part.at[shard_of(-2)], rs.at[3], rs_s.at[3], rs_r.at[3], device(dz=-8))
    go(g_ref, low.at[3], low_s.at[3], low_r.at[3], device(dz=1))

    def to_row(dx, src):
        return remote(src, low.at[dx - 1], low_s.at[dx - 1], low_r.at[dx - 1], device(dx=dx))

    for dx in (1, 2, 3):
        pl.when(x + dx < XN)(to_row(dx, g_ref).start)

    for buf, shift, dst, dz in ((0, 2, 5, 8), (1, 1, 4, 4), (2, -1, 6, -4)):
        arrived(rs.at[buf], rs_s.at[buf], rs_r.at[buf])
        rs[buf] = rs[buf] + part[shard_of(shift)]
        go(rs.at[buf], rs.at[dst], rs_s.at[dst], rs_r.at[dst], device(dz=dz))
    arrived(low.at[3], low_s.at[3], low_r.at[3])
    for dx in (1, 2, 3):
        pl.when(x + dx >= XN)(to_row(dx, low.at[3]).start)
    arrived(con.at[0], con_s.at[0], con_r.at[0])
    pl.when(jnp.logical_not(edge))(beside.wait_recv)
    load_h.wait()
    scale = B ** -0.5
    inside = jnp.where(jnp.logical_or(slab == 0, slab == 3), 0.0, 0.5 * scale).astype(F32)
    level = level_ref[0]
    lane = lax.broadcasted_iota(jnp.int32, (32, B), 1)
    line = lax.broadcasted_iota(jnp.int32, (32, B), 0)
    partner = device(rep_=1 - rep)

    def base_rows(n, _):
        pair = pl.ds(2 * n, 2)
        rows = pl.ds(pl.multiple_of(n * 32, 32), 32)
        contact = (con[0, pair].reshape(32, B).astype(F32) * (0.5 * scale)
                   + con[1, pair].reshape(32, B).astype(F32) * inside)
        diag = lane == line + (rep * H + n * 32)
        base[rep, rows, :] = jnp.where(diag, level, 0.0) + h_ref[rows, :] - contact
        return 0

    lax.fori_loop(0, 8, base_rows, 0)
    go(base.at[rep], base.at[rep], e_s.at[0], e_r.at[0], partner)

    for buf in (3, 4, 6, 5):
        arrived(rs.at[buf], rs_s.at[buf], rs_r.at[buf])
    total = (rs[3] + rs[4] + rs[5] + rs[6] + part[zb]) * (E ** -0.5)

    ft = (zb // 4 + xh) % 2
    row16 = 4 * zc + x
    c_rows = c_ref[row16 // 8, pl.ds(pl.multiple_of((row16 % 8) * 16, 16), 16),
                   pl.ds(pl.multiple_of((zb % 4) * 128, 128), 128)]
    sh, sl = split((B ** -0.5) * c_rows * total)
    shard[0] = sh
    shard[1] = sl
    fm = (xh + rep) % 2

    def column(rep_):
        return 2 * ((ft + rep_) % 2) + core

    xt = column(rep)
    slot_n = nblk.at[rep, zc, zb, xl]
    own = jnp.logical_and(xt == x, core == rep)
    self_copy = pltpu.make_async_copy(shard, slot_n, m_r.at[0, xl])
    same_copy = remote(shard, slot_n, m_s.at[0, 0], m_r.at[0, xl], device(x_=xt, core_=rep))
    shifts = (0, 1, -1, 2, -2)
    for m in (3, 4, 1, 2):
        for other in range(2):
            go(shard, slot_n, m_s.at[m, other], m_r.at[m, xl],
               device(dz=4 * shifts[m], x_=column((rep + other) % 2), core_=rep,
                      rep_=(rep + other) % 2))
    pl.when(own)(self_copy.start)
    pl.when(jnp.logical_not(own))(same_copy.start)
    go(shard, slot_n, m_s.at[0, 1], m_r.at[0, xl],
       device(x_=column(1 - rep), core_=rep, rep_=1 - rep))

    dirs = (1, -1, 2)

    def to_window(block, index):
        for di, dz in enumerate(dirs):
            go(block, block, b_s.at[di, index], b_r.at[di, index], device(dz=dz))

    def own_block(shift):
        return nblk.at[core, zc, shard_of(-shift)]

    for m in range(5):
        block = own_block(shifts[m])
        for xs in range(2):
            arrived(nblk.at[core, zc, shard_of(-shifts[m]), xs], m_s.at[m, 0], m_r.at[m, xs])
        if shifts[m] == 2:
            go(block, block, f_s.at[1], f_r.at[1], device(dz=8))
            go(block, block, f_s.at[0], f_r.at[0], device(dz=4))
        if shifts[m] == -2:
            go(block, block, f_s.at[2], f_r.at[2], device(dz=-4))
        to_window(block, m)
    for d in range(3):
        arrived(low.at[d], low_s.at[d], low_r.at[d])

    def pick_rows(n, _):
        rows = pl.ds(pl.multiple_of(n * 32, 32), 32)
        for f in range(2):
            lw = low[offs[f] - 1, pl.ds(2 * n, 2)].reshape(32, B).astype(F32)
            lsel[rep, f, rows, :] = jnp.where(energy >= offs[f], lw, 0.0).astype(BF16)
        return 0

    lax.fori_loop(0, 8, pick_rows, 0)
    go(lsel.at[rep], lsel.at[rep], e_s.at[1], e_r.at[1], partner)
    far = (3, -3, 4)
    for n, (shift, sem) in enumerate(((3, 0), (-3, 2), (4, 1))):
        block = own_block(shift)
        arrived(block, f_s.at[sem], f_r.at[sem])
        to_window(block, 5 + n)
    sibling = device(core_=1 - core)
    go(nblk.at[core, zc], nblk.at[core, zc], sib_s.at[0], sib_r.at[0], sibling)
    for di, dz in enumerate(dirs):
        zs = (z - dz + ZN) % ZN
        ks, js = zs // 4, zs % 4
        for index, shift in enumerate(shifts + far):
            kk = (ks - shift + 8) % 8
            arrived(nblk.at[core, js, kk], b_s.at[di, index], b_r.at[di, index])
        go(nblk.at[core, js], nblk.at[core, js], sib_s.at[1 + di], sib_r.at[1 + di], sibling)
    for n, dz in enumerate((0,) + dirs):
        js = (z - dz + ZN) % 4
        arrived(nblk.at[1 - core, js], sib_s.at[n], sib_r.at[n])

    def assemble(n, _):
        for p in range(2):
            for xs in range(2):
                for cb in range(4):
                    kk = 4 * ((fm + p) % 2) + cb
                    rows = pl.ds(pl.multiple_of(n * 64 + 32 * p + 16 * xs, 16), 16)
                    nhi[rows, 128 * cb:128 * cb + 128] = nblk[n // 4, n % 4, kk, xs, 0]
                    nlo[rows, 128 * cb:128 * cb + 128] = nblk[n // 4, n % 4, kk, xs, 1]
        return 0

    lax.fori_loop(0, 8, assemble, 0)

    arrived(cbuf, cs_s.at[0], cs_r.at[0])
    local = xl == core
    cw = cbuf[...].reshape(H, B)
    count = ssteps_ref[fm]
    u1 = product(cw, nhi[...], nlo[...])
    u2 = product(u1, nhi[...], nlo[...])
    u3 = product(u2, nhi[...], nlo[...])
    w1 = cw - u1
    w2 = w1 + (u2 - u3)
    wown[...] = jnp.where(count >= 2, w2, jnp.where(count >= 1, w1, cw)).astype(BF16)
    slot_w = wbuf.at[fm, core]
    w_self = pltpu.make_async_copy(wown, slot_w, w_r.at[fm, core])
    w_sib = remote(wown, slot_w, w_s.at[0], w_r.at[fm, core], device(core_=xl))
    for n, dev in enumerate((device(dx=1, core_=xl), device(dx=-1, core_=xl),
                             device(core_=xl, rep_=1 - rep))):
        go(wown, slot_w, w_s.at[1 + n], w_r.at[fm, core], dev)
    pl.when(local)(w_self.start)
    pl.when(jnp.logical_not(local))(w_sib.start)

    for n, buf in enumerate((base, lsel)):
        arrived(buf.at[1 - rep], e_s.at[n], e_r.at[n])
    for f in range(2):
        for half in range(2):
            arrived(wbuf.at[f, half], w_s.at[0], w_r.at[f, half])

    def operator(n, carry):
        r = n // 8
        rows = pl.ds(pl.multiple_of((n % 8) * 32, 32), 32)
        self_energy = (lsel[r, 0, rows, :].astype(F32) * wbuf[0, r, rows, :].astype(F32)
                       + lsel[r, 1, rows, :].astype(F32) * wbuf[1, r, rows, :].astype(F32)) * scale
        dyson = base[r, rows, :] - self_energy
        diag = lane == line + n * 32
        dd = jnp.sum(jnp.where(diag, dyson, 0.0), axis=1, keepdims=True)
        iv = 1.0 / dd
        kk = jnp.where(diag, 0.0, dyson * iv)
        kf[r, rows, :] = kk
        kh, kl = split(kk)
        kbuf[r, 0, rows, :] = kh
        kbuf[r, 1, rows, :] = kl
        return carry + jnp.sum(jnp.where(diag, iv, 0.0), axis=0, keepdims=True)

    inv_all = lax.fori_loop(0, 16, operator, jnp.zeros((1, B), F32))
    for f in range(2):
        w_ref[f] = wbuf[f, rep]

    zbuf[...] = (product(kf[rep, :, 0:H], kbuf[0, 0], kbuf[0, 1])
                 + product(kf[rep, :, H:B], kbuf[1, 0], kbuf[1, 1]))
    cube = (product(zbuf[:, 0:H], kbuf[0, 0], kbuf[0, 1])
            + product(zbuf[:, H:B], kbuf[1, 0], kbuf[1, 1]))
    twice = gsteps_ref[0] >= 2
    full_lane = lax.broadcasted_iota(jnp.int32, (H, B), 1)
    full_line = lax.broadcasted_iota(jnp.int32, (H, B), 0) + rep * H
    ident = jnp.where(full_lane == full_line, 1.0, 0.0).astype(F32)
    first = ident - kf[rep]
    out_ref[...] = jnp.where(twice, first + (zbuf[...] - cube), first)
    inv_ref[...] = jnp.broadcast_to(inv_all, (8, B))

    for copy in pending:
        copy.wait_send()
    for dx in (1, 2, 3):
        to_row(dx, g_ref).wait_send()
    pl.when(jnp.logical_not(own))(same_copy.wait_send)
    pl.when(jnp.logical_not(local))(w_sib.wait_send)
    pl.when(c_there)(c_same.wait_send)
    pl.when(jnp.logical_not(edge))(beside.wait_send)
    pl.when(holds)(c_other.wait_send)


def body(green_blocks, occupation, offsets, coulomb, hamiltonian, onsite_level, green_steps,
         screen_steps):
    smem = pl.BlockSpec(memory_space=pltpu.SMEM)
    hbm = pl.BlockSpec(memory_space=pl.ANY)
    vmem = pl.BlockSpec(memory_space=pltpu.VMEM)
    dma = pltpu.SemaphoreType.DMA
    sems = []
    for shape in ((5, 4), (5, 4), (4,), (2,), (2,), (7,), (5, 2), (3,), (3, 8), (4,)):
        sems += [dma(shape), dma(shape)]
    sems += [dma((4,)), dma((2, 2)), dma((2,)), dma((2,)), dma((3,)),
             pltpu.SemaphoreType.REGULAR]
    green, screened, scales = pl.pallas_call(
        kernel,
        out_shape=(
            jax.ShapeDtypeStruct((H, B), F32),
            jax.ShapeDtypeStruct((2, H, B), BF16),
            jax.ShapeDtypeStruct((8, B), F32),
        ),
        in_specs=[smem] * 5 + [hbm] * 3,
        out_specs=(vmem, vmem, vmem),
        scratch_shapes=[
            pltpu.VMEM((16, 16, B), BF16),
            pltpu.VMEM((2, 128, B), F32),
            pltpu.VMEM((H, B), F32),
            pltpu.VMEM((20, 16, B), BF16),
            pltpu.VMEM((20, 8, 128), F32),
            pltpu.VMEM((4, 16, 16, B), BF16),
            pltpu.VMEM((2, 16, 16, B), BF16),
            pltpu.VMEM((2, 128, B), F32),
            pltpu.VMEM((8, 16, 128), F32),
            pltpu.VMEM((7, 16, 128), F32),
            pltpu.VMEM((2, 16, 128), BF16),
            pltpu.VMEM((2, 4, 8, 2, 2, 16, 128), BF16),
            pltpu.VMEM((B, B), BF16),
            pltpu.VMEM((B, B), BF16),
            pltpu.VMEM((H, B), BF16),
            pltpu.VMEM((2, 2, H, B), BF16),
            pltpu.VMEM((2, H, B), F32),
            pltpu.VMEM((2, 2, H, B), BF16),
            pltpu.VMEM((2, H, B), F32),
            pltpu.VMEM((2, 2, H, B), BF16),
            pltpu.VMEM((H, B), F32),
        ] + sems,
        compiler_params=pltpu.CompilerParams(
            collective_id=0, has_side_effects=True, vmem_limit_bytes=62 << 20
        ),
        name="gw_step",
    )(
        occupation, offsets, onsite_level, green_steps, screen_steps,
        green_blocks.reshape(16, 16, B), coulomb.reshape(2, 128, B), hamiltonian.reshape(H, B),
    )
    green = green * scales[0:1]
    return green.reshape(1, 1, H, B), screened.reshape(2, 1, H, B)


def solution(mesh):
    return jax.shard_map(
        body,
        mesh=mesh,
        in_specs=(
            P("energy", "slab", "rep", None),
            P("energy"),
            P(),
            P("slab", "rep", None),
            P("slab", "rep", None),
            P("energy"),
            P("energy"),
            P(),
        ),
        out_specs=(P("energy", "slab", "rep", None), P(None, "slab", "rep", None)),
        check_vma=False,
    )
```
